128 devices in a mesh: leaf: 16 (over x, y), sub: 8 (over z, core).
Axes of the slice: x: 4, y: 4, z: 4, core: 2. Of those that a mesh axis runs over, the one named last changes fastest.
Arguments:
- charges: bfloat16 [32, 2097152], P(None, ('leaf', 'sub')), may hold values from -0.59765625 to 0.59765625
- points: float32 [3, 2097152], P(None, ('leaf', 'sub')), as said below
- basis: bfloat16 [16384, 64, 128], P(('leaf', 'sub')), may hold values from -0.5 to 0.5
- transfer: float32 [2, 64, 64], replicated, may hold values from -0.625 to 0.625
- near_list: int32 [16384, 8], P(('leaf', 'sub')), may hold values from -1 to 16383, as said below
- coupling_list: int32 [16384, 8], P(('leaf', 'sub')), may hold values from -1 to 16383, as said below
Outputs:
- potential: float32 [32, 2097152], P(None, ('leaf', 'sub'))
The draws below stay inside these ranges and needn't reach their ends.
Inputs may be any that keep to these rules, and one draw needn't show every extreme that they name: `near_list`: every live slot of row i holds a leaf j with |j - i| <= 64 whose unit box touches the box of leaf i (the box corners differ by at most 1 in every coordinate); slot 0 holds i itself, slot 1 the leaf whose index differs from i in the lowest bit, slot 2 the leaf i - 4 (i + 4 where i < 4), slot 3 the leaf i + 4 (i - 4 where i + 4 >= 16384); other slots may repeat leaves; empty slots hold -1 and come after the live ones; at least four slots of every row are live, and how many are live varies from device to device. `coupling_list`: every live slot of row i holds a leaf j with 1 <= |j - i| <= 64 whose unit box does not touch the box of leaf i (the box corners differ by 2 or more in some coordinate); slot 1 holds a leaf exactly 64 away from i; other slots may repeat leaves; empty slots hold -1 and come after the live ones; at least two slots of every row are live, and how many are live varies from device to device. The points of leaf c lie in the unit box whose lower corner is (c % 2, (c // 2) % 2, c // 4).
All inputs are finite; a program needn't handle non-finite values.
Results may differ from the reference program's by a relative error of at most 0.00065.
The reference program's roundings to bfloat16 on the way (of `near_tile` and `down_leaf`) count: a program that leaves them out, or rounds other values in their place, can miss the bound.
Values may be sent and summed in bfloat16 or wider, within the bound.
A program may use at most 128 MiB of HBM per device.

```python
import math
import jax
import jax.numpy as jnp
from jax import lax

P_SIZE = 128
K = 64
R = 32
LD = 128
NEAR = 8
COUP = 8
NBAND = 64
LEAVES = 16384
POINTS = 2097152


def axis_extent(axis_id):
    return 2 if axis_id < 2 else LEAVES // 4


def box_coords(leaf_ids):
    return [leaf_ids % 2, leaf_ids // 2 % 2, leaf_ids // 4]


def box_index(coords):
    return coords[0] + 2 * coords[1] + 4 * coords[2]


def live_counts(key, slots, least):
    leaf_ids = jnp.arange(LEAVES, dtype=jnp.int32)
    key_cap, key_count = jax.random.split(key, 2)
    owners = LEAVES // LD
    caps = jax.random.randint(key_cap, (owners,), least, slots + 1)
    caps = caps.at[0].set(least)
    owner_of = leaf_ids // LD
    counts = jnp.minimum(jax.random.randint(key_count, (LEAVES,), least, slots + 1), caps[owner_of])
    return jnp.where(owner_of == owners - 1, slots, counts)


def draw_near_list(key, part):
    key = jax.random.fold_in(key, 21)
    key_step, key_count = jax.random.split(key, 2)
    leaf_ids = jnp.arange(LEAVES, dtype=jnp.int32)[:, None]
    column = jnp.arange(NEAR, dtype=jnp.int32)[None, :]
    own = box_coords(jnp.broadcast_to(leaf_ids, (LEAVES, NEAR)))
    steps_drawn = jax.random.randint(key_step, (3, LEAVES, NEAR), -1, 2)
    moved = [own[axis_id] + steps_drawn[axis_id] for axis_id in range(3)]
    inside = jnp.ones((LEAVES, NEAR), bool)
    for axis_id in range(3):
        inside = inside & (moved[axis_id] >= 0) & (moved[axis_id] < axis_extent(axis_id))
    clamped = [jnp.clip(moved[axis_id], 0, axis_extent(axis_id) - 1) for axis_id in range(3)]
    target = box_index(clamped)
    sibling = leaf_ids + 1 - 2 * (leaf_ids % 2)
    below = jnp.where(leaf_ids >= 4, leaf_ids - 4, leaf_ids + 4)
    above = jnp.where(leaf_ids + 4 < LEAVES, leaf_ids + 4, leaf_ids - 4)
    valid = inside & (target != leaf_ids) & (jnp.abs(target - leaf_ids) <= NBAND)
    target = jnp.where(valid, target, sibling)
    target = jnp.where(column == 3, above, target)
    target = jnp.where(column == 2, below, target)
    target = jnp.where(column == 1, sibling, target)
    target = jnp.where(column == 0, leaf_ids, target)
    counts = live_counts(key_count, NEAR, 4)
    return jnp.where(column < counts[:, None], target, -1).astype(jnp.int32)


def draw_coupling_list(key, part):
    key = jax.random.fold_in(key, 22)
    key_offset, key_sign, key_count = jax.random.split(key, 3)
    leaf_ids = jnp.arange(LEAVES, dtype=jnp.int32)[:, None]
    column = jnp.arange(COUP, dtype=jnp.int32)[None, :]
    band_bit = leaf_ids // NBAND % 2
    exact = jnp.where(band_bit == 0, leaf_ids + NBAND, leaf_ids - NBAND)
    distance = jax.random.randint(key_offset, (LEAVES, COUP), 1, NBAND + 1)
    signs = 2 * jax.random.randint(key_sign, (LEAVES, COUP), 0, 2) - 1
    target = leaf_ids + signs * distance
    target = jnp.where((target < 0) | (target >= LEAVES), leaf_ids - signs * distance, target)
    own = box_coords(jnp.broadcast_to(leaf_ids, (LEAVES, COUP)))
    other = box_coords(target)
    apart = jnp.zeros((LEAVES, COUP), bool)
    for axis_id in range(3):
        apart = apart | (jnp.abs(own[axis_id] - other[axis_id]) >= 2)
    target = jnp.where(apart, target, exact)
    target = jnp.where(column == 1, exact, target)
    counts = live_counts(key_count, COUP, 2)
    return jnp.where(column < counts[:, None], target, -1).astype(jnp.int32)


def draw_points(key, part):
    key = jax.random.fold_in(key, 23)
    leaf_ids = jnp.arange(LEAVES, dtype=jnp.int32)
    corner = jnp.stack(box_coords(leaf_ids)).astype(jnp.float32)
    spread = jax.random.uniform(key, (3, LEAVES, P_SIZE), jnp.float32)
    return (corner[:, :, None] + spread).reshape(3, LEAVES * P_SIZE)


def block_scale(stream_key, dims, cuts, smallest, top_value):
    def one(position, shards_of):
        draws = jax.random.uniform(jax.random.fold_in(jax.random.fold_in(stream_key, 6), position), (shards_of,), jnp.float32, smallest / len(cuts), top_value / len(cuts))
        return jnp.repeat(jnp.exp(draws), dims[position] // shards_of).reshape((-1,) + (1,) * (len(dims) - position - 1))

    factor_of = one(*cuts[0])
    for cut in cuts[1:]:
        factor_of = factor_of * one(*cut)
    return factor_of


def gaussian(stream_key, shape, width, bound, cuts=(), kind=jnp.bfloat16):
    array = jax.random.normal(stream_key, shape, jnp.float32) * width
    if len(cuts) > 0:
        array = block_scale(stream_key, shape, cuts, -0.22, 0.18) * array
    return jnp.clip(array, min=-bound, max=bound).astype(kind)


def setup_inputs(seed: int = 0) -> dict:
    seeds = jax.random.split(jax.random.key(seed), 7)
    charges = gaussian(seeds[0], (R, POINTS), 0.1, 0.59765625, ((1, 128),))
    points = draw_points(jax.random.fold_in(seeds[6], 71), 0)
    basis = gaussian(seeds[2], (LEAVES, K, P_SIZE), P_SIZE ** -0.5, 0.5, ((0, 128),))
    transfer = gaussian(seeds[3], (2, K, K), (K + K // 2) ** -0.5, 0.625, (), jnp.float32)
    near_list = draw_near_list(jax.random.fold_in(seeds[6], 71), 0)
    coupling_list = draw_coupling_list(jax.random.fold_in(seeds[6], 71), 0)
    return {"charges": charges, "points": points, "basis": basis, "transfer": transfer, "near_list": near_list, "coupling_list": coupling_list}


LENGTH_SCALE = 2.0
NUGGET_VARIANCE = 1.0
HIGHEST = lax.Precision.HIGHEST

def unit_nodes():
    index_row = jnp.arange(64, dtype=jnp.int32)

    def axis_value(digit):
        return jnp.cos((2.0 * digit.astype(jnp.float32) + 1.0) * (math.pi / 8.0))
    return jnp.stack([axis_value(index_row // 16), axis_value(index_row // 4 % 4), axis_value(index_row % 4)])

def covariance(first, second):
    separation = first[..., :, None] - second[..., None, :]
    return jnp.exp(-jnp.sqrt(lax.optimization_barrier(jnp.sum(separation * separation, axis=0))) / LENGTH_SCALE)

def cluster_nodes(centers, radii, reference_nodes):
    extra = (1,) * (centers.ndim - 1)
    shaped = reference_nodes.reshape((3,) + extra + (reference_nodes.shape[1],))
    return centers[..., None] + radii[None, ..., None] * shaped

def leaf_shapes(leaf_points):
    centers = lax.optimization_barrier(jnp.mean(leaf_points, axis=2))
    offsets = leaf_points - centers[:, :, None]
    radii = lax.optimization_barrier(jnp.max(jnp.sqrt(lax.optimization_barrier(jnp.sum(offsets * offsets, axis=0))), axis=1))
    return (centers, radii)

def merge_shapes(centers, radii):
    paired = centers.reshape(3, -1, 2)
    spread = radii.reshape(-1, 2)
    separation = paired[:, :, 0] - paired[:, :, 1]
    joined = 0.5 * (paired[:, :, 0] + paired[:, :, 1])
    return (joined, jnp.maximum(spread[:, 0], spread[:, 1]) + 0.5 * jnp.sqrt(lax.optimization_barrier(jnp.sum(separation * separation, axis=0))))

def merge_coefficients(coefficient, transfer):
    paired = coefficient.reshape(coefficient.shape[0], -1, 2, coefficient.shape[2])
    return jnp.einsum('rcsk,skj->rcj', paired, transfer, precision=HIGHEST)

def descend(downward, transfer):
    spread = jnp.einsum('rcj,skj->rcsk', downward, transfer, precision=HIGHEST)
    return spread.reshape(downward.shape[0], -1, downward.shape[2])

def sibling_coupling(coefficient, centers, radii, reference_nodes):
    nodes = cluster_nodes(centers, radii, reference_nodes)
    paired = nodes.reshape(3, -1, 2, nodes.shape[2])
    kernel_tile = covariance(paired[:, :, 0], paired[:, :, 1])
    coef_pairs = coefficient.reshape(coefficient.shape[0], -1, 2, coefficient.shape[2])
    to_left = jnp.einsum('rcq,cpq->rcp', coef_pairs[:, :, 1], kernel_tile, precision=HIGHEST)
    to_right = jnp.einsum('rcp,cpq->rcq', coef_pairs[:, :, 0], kernel_tile, precision=HIGHEST)
    return jnp.stack([to_left, to_right], axis=2).reshape(coefficient.shape)

def listed_coupling(all_coef, all_centers, all_radii, own_centers, own_radii, slot_rows, reference_nodes):
    is_live = slot_rows >= 0
    safe_rows = jnp.where(is_live, slot_rows, 0).astype(jnp.int32)
    own_nodes = cluster_nodes(own_centers, own_radii, reference_nodes)
    far_nodes = cluster_nodes(jnp.take(all_centers, safe_rows, axis=1), jnp.take(all_radii, safe_rows, axis=0), reference_nodes)
    kernel_tile = covariance(own_nodes[:, :, None, :], far_nodes) * is_live.astype(jnp.float32)[:, :, None, None]
    far_coef = jnp.take(all_coef, safe_rows, axis=1)
    return jnp.einsum('wspq,rwsq->rwp', kernel_tile, far_coef, precision=HIGHEST)

def near_tile(all_x, all_points, own_x, own_points, slot_rows):
    is_live = slot_rows >= 0
    safe_rows = jnp.where(is_live, slot_rows, 0).astype(jnp.int32)
    far_points = jnp.take(all_points, safe_rows, axis=1)
    kernel_tile = (covariance(own_points[:, :, None, :], far_points) * is_live.astype(jnp.float32)[:, :, None, None]).astype(jnp.bfloat16)
    far_x = jnp.take(all_x, safe_rows, axis=1)
    summed = jnp.einsum('wspq,rwsq->rwp', kernel_tile.astype(jnp.float32), far_x.astype(jnp.float32))
    return summed + NUGGET_VARIANCE * own_x.astype(jnp.float32)

def blocked(function, total_rows, block_size):
    starts = jnp.arange(total_rows // block_size, dtype=jnp.int32) * block_size
    pieces = lax.map(function, starts)
    return jnp.moveaxis(pieces, 0, 1).reshape(pieces.shape[1], total_rows, pieces.shape[3])

def reference(charges, points, basis, transfer, near_list, coupling_list):
    reference_nodes = unit_nodes()
    leaf_x = charges.reshape(R, LEAVES, P_SIZE)
    leaf_points = points.reshape(3, LEAVES, P_SIZE)

    def near_block(start_leaf):
        return near_tile(leaf_x, leaf_points, lax.dynamic_slice_in_dim(leaf_x, start_leaf, 64, 1), lax.dynamic_slice_in_dim(leaf_points, start_leaf, 64, 1), lax.dynamic_slice_in_dim(near_list, start_leaf, 64, 0))
    near = blocked(near_block, LEAVES, 64)
    coefficient = jnp.einsum('rcp,ckp->rck', leaf_x.astype(jnp.float32), basis.astype(jnp.float32))
    centers, radii = leaf_shapes(leaf_points)

    def couple_block(start_leaf):
        return listed_coupling(coefficient, centers, radii, lax.dynamic_slice_in_dim(centers, start_leaf, 64, 1), lax.dynamic_slice_in_dim(radii, start_leaf, 64, 0), lax.dynamic_slice_in_dim(coupling_list, start_leaf, 64, 0), reference_nodes)
    leaf_couple = blocked(couple_block, LEAVES, 64)
    levels = [(coefficient, centers, radii)]
    while levels[-1][0].shape[1] > 1:
        last_coef, last_centers, last_radii = levels[-1]
        joined_centers, joined_radii = merge_shapes(last_centers, last_radii)
        levels.append((merge_coefficients(last_coef, transfer), joined_centers, joined_radii))
    downward = jnp.zeros((R, 1, K), jnp.float32)
    for level_index in range(len(levels) - 2, 0, -1):
        level_coef, level_centers, level_radii = levels[level_index]
        downward = descend(downward, transfer) + sibling_coupling(level_coef, level_centers, level_radii, reference_nodes)
    downward = descend(downward, transfer) + leaf_couple
    down_leaf = downward.astype(jnp.bfloat16)
    far = jnp.einsum('rck,ckp->rcp', down_leaf.astype(jnp.float32), basis.astype(jnp.float32))
    return (near + far).reshape(R, POINTS)
```

```python
import math

import jax
import jax.numpy as jnp
from jax import lax
from jax.experimental import pallas as pl
from jax.experimental.pallas import tpu as pltpu
from jax.sharding import PartitionSpec as P

F32, BF16 = jnp.float32, jnp.bfloat16
PT = 128
K = 64
R = 32
LD = 128
REACH = 64
GRP = 4
GW = GRP * PT
GROUPS = LD // GRP
EXT = (GROUPS + 2) * GW
FEAT = 48
SCALE = math.log2(math.e) / 2.0
TINY = 1e-30
MESH = pl.DeviceIdType.MESH


def dot(a, b):
    return lax.dot_general(a, b, (((1,), (0,)), ((), ())), preferred_element_type=F32)


def dot_nt(a, b):
    return lax.dot_general(a, b, (((1,), (1,)), ((), ())), preferred_element_type=F32)


def dot_tn(a, b):
    return lax.dot_general(a, b, (((0,), (0,)), ((), ())), preferred_element_type=F32)


def split2(x):
    high = x.astype(BF16)
    return high, (x - high.astype(F32)).astype(BF16)


def dot3(a, b_high, b_low):
    high, low = split2(a)
    return dot(high, b_high) + (dot(high, b_low) + dot(low, b_high))


def from_square(d2):
    x = jnp.maximum(d2, TINY)
    return jnp.exp2(-(x * lax.rsqrt(x)))


def features(coords, axis):
    high = coords.astype(BF16).astype(F32)
    low = (coords - high).astype(BF16).astype(F32)
    kept = high + low
    norm = jnp.sum(kept * kept, axis=axis, keepdims=True)
    n1 = norm.astype(BF16).astype(F32)
    n2 = (norm - n1).astype(BF16).astype(F32)
    n3 = norm - n1 - n2
    row = lax.broadcasted_iota(jnp.int32, coords.shape, axis)
    norms = jnp.where(row == 0, n1, jnp.where(row == 1, n2, jnp.where(row == 2, n3, 0.0)))
    ones = jnp.where(row < 3, 1.0, 0.0)
    high2, low2 = -2.0 * high, -2.0 * low
    u = jnp.concatenate([high, high, low, low, norms, ones], axis=axis)
    v = jnp.concatenate([high2, low2, high2, low2, ones, norms], axis=axis)
    return u, v


def unit_rows():
    row = lax.broadcasted_iota(jnp.int32, (8, 128), 0)
    index = lax.broadcasted_iota(jnp.int32, (8, 128), 1) % K
    digit = jnp.where(row == 0, index // 16, jnp.where(row == 1, index // 4 % 4, index % 4))
    big, small = math.cos(math.pi / 8.0), math.cos(3.0 * math.pi / 8.0)
    value = jnp.where(
        digit == 0, big, jnp.where(digit == 1, small, jnp.where(digit == 2, -small, -big))
    )
    return jnp.where(row < 3, value, 0.0).astype(F32)


def lower_lanes(shape):
    return lax.broadcasted_iota(jnp.int32, shape, len(shape) - 1) < K


def halves(x):
    paired = x.reshape((x.shape[0] // 2, 2) + x.shape[1:])
    return paired[:, 0], paired[:, 1]


def side_by_side(x):
    left, right = halves(x)
    return jnp.where(lower_lanes(left.shape), left, right)


def merge_shapes(centers, radii):
    c0, c1 = halves(centers)
    r0, r1 = halves(radii)
    gap = c0 - c1
    reach = jnp.sqrt(jnp.sum(gap * gap, axis=1, keepdims=True))
    return 0.5 * (c0 + c1), jnp.maximum(r0, r1) + 0.5 * reach


def pair_coords(centers, radii, units):
    c0, c1 = halves(centers)
    r0, r1 = halves(radii)
    half = 0.5 * (c0 - c1)
    left = lower_lanes(half.shape)
    return SCALE * (jnp.where(left, half, -half) + jnp.where(left, r0, r1) * units[None])


def couple_pair(coefs, coords):
    columns = jnp.transpose(coords)
    d2 = None
    for k in range(3):
        gap = columns[:, k : k + 1] - coords[k : k + 1, :]
        d2 = gap * gap if d2 is None else d2 + gap * gap
    across = (lax.broadcasted_iota(jnp.int32, (128, 128), 0) < K) != lower_lanes((128, 128))
    tile = jnp.where(across, from_square(d2), 0.0)
    tile_high, tile_low = split2(tile)
    return dot3(coefs, tile_high, tile_low)


def kernel(
    nl, ns,
    charges, points, basis, transfer, near_list, coupling_list,
    out,
    p8, xe, oe, ua, va, vb, weight,
    leaf_pts, centers, radii, pairs, pair_co, sib,
    up_pair, v_left, v_right, c_left, c_right, lc,
    send_coef, halo_coef, send_shape, halo_shape,
    root, got_sub, root_b, got_leaf, path_pair, path_co, e0,
    near_send, near_recv, coup_send, coup_recv, sub_send, sub_recv, leaf_send, leaf_recv,
):
    leaf_id, sub_id = lax.axis_index("leaf"), lax.axis_index("sub")
    count = nl * ns
    me = leaf_id * ns + sub_id
    right, left = lax.rem(me + 1, count), lax.rem(me + count - 1, count)
    left_dev = (left // ns, lax.rem(left, ns))
    right_dev = (right // ns, lax.rem(right, ns))
    sub_devs = [(leaf_id, lax.rem(sub_id + o, ns)) for o in range(1, ns)]
    leaf_devs = [(lax.rem(leaf_id + o, nl), sub_id) for o in range(1, nl)]
    barrier = pltpu.get_barrier_semaphore()
    partners = [left_dev, right_dev] + sub_devs + leaf_devs
    for device in partners:
        pl.semaphore_signal(barrier, inc=1, device_id=device, device_id_type=MESH)

    def send(src, dst, send_sem, recv_sem, device):
        copy = pltpu.make_async_remote_copy(
            src_ref=src, dst_ref=dst, send_sem=send_sem, recv_sem=recv_sem,
            device_id=device, device_id_type=MESH,
        )
        copy.start()
        return copy

    first = me * LD
    units = unit_rows()
    lane_half = lower_lanes((R, 128))

    p8[3:8, GW : EXT - GW] = jnp.zeros((5, LD * PT), F32)
    p8[0:3, GW : EXT - GW] = points[...]

    pl.semaphore_wait(barrier, len(partners))
    copies = []
    copies.append(send(charges.at[:, pl.ds(0, GW)], xe.at[:, pl.ds(EXT - GW, GW)],
                       near_send.at[0], near_recv.at[0], left_dev))
    copies.append(send(charges.at[:, pl.ds(LD * PT - GW, GW)], xe.at[:, pl.ds(0, GW)],
                       near_send.at[1], near_recv.at[1], right_dev))
    copies.append(send(p8.at[:, pl.ds(GW, GW)], p8.at[:, pl.ds(EXT - GW, GW)],
                       near_send.at[2], near_recv.at[2], left_dev))
    copies.append(send(p8.at[:, pl.ds(EXT - 2 * GW, GW)], p8.at[:, pl.ds(0, GW)],
                       near_send.at[3], near_recv.at[3], right_dev))
    near_copies = copies

    for c in range(LD):
        leaf_pts[c] = p8[:, GW + c * PT : GW + (c + 1) * PT]

    @pl.loop(0, LD // 16)
    def _(block):
        rows = pl.ds(block * 16, 16)
        pts = leaf_pts[rows]
        center = jnp.mean(pts, axis=2, keepdims=True)
        off = pts - center
        far = jnp.max(jnp.sum(off * off, axis=1, keepdims=True), axis=2, keepdims=True)
        centers[rows] = jnp.broadcast_to(center, pts.shape)
        radii[rows] = jnp.broadcast_to(jnp.sqrt(far), pts.shape)

    row8 = lax.broadcasted_iota(jnp.int32, (8, 128), 0)
    lane8 = lax.broadcasted_iota(jnp.int32, (8, 128), 1)

    packed = jnp.zeros((8, 128), F32)
    for c in range(LD):
        packed = jnp.where(lane8 == c, jnp.where(row8 < 3, centers[c], radii[c]), packed)
    send_shape[...] = packed

    @pl.loop(0, LD // 16)
    def _(block):
        for s in range(8):
            m = block * 8 + s
            x = charges[:, pl.ds(pl.multiple_of(m * 256, 256), 256)]
            stacked = jnp.concatenate([x[:, :128], x[:, 128:]], axis=0)
            both = basis[pl.ds(2 * m, 2)].reshape(2 * K, PT)
            product = dot_nt(stacked, both)
            pair = jnp.where(lane_half, product[:R], product[R:])
            pairs[m] = pair
            send_coef[m] = pair.astype(BF16)

    half_pairs = REACH // 2
    coup_copies = [
        send(send_coef.at[pl.ds(0, half_pairs)], halo_coef.at[1],
             coup_send.at[0], coup_recv.at[0], left_dev),
        send(send_coef.at[pl.ds(half_pairs, half_pairs)], halo_coef.at[0],
             coup_send.at[1], coup_recv.at[1], right_dev),
        send(send_shape, halo_shape.at[1], coup_send.at[2], coup_recv.at[2], left_dev),
        send(send_shape, halo_shape.at[0], coup_send.at[3], coup_recv.at[3], right_dev),
    ]

    t0, t1 = transfer[0], transfer[1]
    up = jnp.concatenate([t0, t1], axis=0)
    up_high, up_low = split2(jnp.concatenate([up, up], axis=1))
    down = jnp.concatenate([jnp.transpose(t0), jnp.transpose(t1)], axis=1)
    down_high, down_low = split2(jnp.concatenate([down, down], axis=0))

    def lift(pair_block):
        n = pair_block.shape[0]
        return dot3(pair_block.reshape(n * R, 128), up_high, up_low).reshape(n, R, 128)

    level_cen, level_rad = centers[...], radii[...]
    offset, n = 0, LD // 2
    block = pairs[pl.ds(0, n)]
    while n > 1:
        block = side_by_side(lift(block))
        level_cen, level_rad = merge_shapes(level_cen, level_rad)
        offset += n
        n //= 2
        pairs[pl.ds(offset, n)] = block
        pair_co[pl.ds(offset - LD // 2, n)] = pair_coords(level_cen, level_rad, units)
    root_coef = lift(block)[0]
    root_cen, root_rad = merge_shapes(level_cen, level_rad)

    def packed_shape(cen, rad):
        return jnp.where(row8 < 3, cen, rad)

    def unpacked_shape(shape):
        rows = lax.broadcasted_iota(jnp.int32, shape.shape, 1)
        cen = jnp.where(rows < 3, shape, 0.0)
        rad = jnp.sum(jnp.where(rows == 3, shape, 0.0), axis=1, keepdims=True)
        return cen, jnp.broadcast_to(rad, shape.shape)

    root[0:R, :] = root_coef
    root[R : R + 8, :] = packed_shape(root_cen[0], root_rad[0])
    sub_copies = [
        send(root, got_sub.at[sub_id], sub_send.at[o], sub_recv.at[o], device)
        for o, device in enumerate(sub_devs)
    ]
    got_sub[sub_id] = root[...]

    @pl.loop(0, 21)
    def _(i):
        for s in range(3):
            sib[i * 3 + s] = couple_pair(pairs[LD // 2 + i * 3 + s], pair_co[i * 3 + s])

    xe[:, GW : EXT - GW] = charges[...]
    oe[:, GW : EXT - GW] = charges[...].astype(F32)
    leaf_row = lax.broadcasted_iota(jnp.int32, (LD, 1), 0)
    base = first + (leaf_row // GRP) * GRP - GRP
    listed = near_list[...]
    relative = jnp.where(listed >= 0, listed - base, -1)
    weight[...] = jnp.zeros_like(weight)
    for k in range(3 * GRP):
        times = jnp.sum(jnp.where(relative == k, 1.0, 0.0), axis=1, keepdims=True)
        weight[k, GRP : GRP + LD, :] = jnp.broadcast_to(times, (LD, 128))

    for copy in near_copies:
        copy.wait()

    @pl.loop(0, GROUPS + 2)
    def _(g):
        lanes = pl.ds(pl.multiple_of(g * GW, GW), GW)
        row = lax.broadcasted_iota(jnp.int32, (8, GW), 0)
        z0 = (me * GROUPS + g - 1).astype(F32)
        corner = jnp.where(row == 2, z0, jnp.where(row < 2, 1.0, 0.0))
        low = p8[:, lanes] - corner
        shift = jnp.where(row == 2, 1.0, 0.0)
        u, v = features(SCALE * (low - shift), 0)
        ua[:, lanes] = u.astype(BF16)
        va[:, lanes] = v.astype(BF16)
        vb[:, lanes] = features(SCALE * low, 0)[1].astype(BF16)

    oe[:, 0:GW] = jnp.zeros((R, GW), F32)
    oe[:, EXT - GW : EXT] = jnp.zeros((R, GW), F32)

    @pl.loop(0, GROUPS + 1)
    def _(g):
        here = pl.ds(pl.multiple_of(g * GW, GW), GW)
        there = pl.ds(pl.multiple_of(g * GW + GW, GW), GW)
        u = ua[:, here]
        v = jnp.concatenate([va[:, here], vb[:, there]], axis=1)
        x = jnp.concatenate([xe[:, here], xe[:, there]], axis=1)
        total = [oe[:, here][:, j * PT : (j + 1) * PT] for j in range(GRP)]
        total += [oe[:, there][:, j * PT : (j + 1) * PT] for j in range(GRP)]

        def times(target, source):
            k = source + GRP if target < GRP else source
            return weight[k, pl.ds(g * GRP + target, 1), :]

        for i in range(GRP):
            d2 = dot_tn(u[:, i * PT : (i + 1) * PT], v[:, i * PT :])
            tile = from_square(d2).astype(BF16)
            part = dot(x[:, i * PT : (i + 1) * PT], tile)
            for j in range(i, 2 * GRP):
                at = (j - i) * PT
                total[j] = total[j] + times(j, i) * part[:, at : at + PT]
                if j > i:
                    back = dot_nt(x[:, j * PT : (j + 1) * PT], tile[:, at : at + PT])
                    total[i] = total[i] + times(i, j) * back
        oe[:, here] = jnp.concatenate(total[:GRP], axis=1)
        oe[:, there] = jnp.concatenate(total[GRP:], axis=1)

    def climb(got, width, level0, index):
        coefs = got[:, 0:R, :]
        cen, rad = unpacked_shape(got[:, R : R + 8, :])
        level = level0
        while width > 1:
            two = side_by_side(coefs)
            path_pair[level, pl.ds(0, width // 2)] = two
            path_co[level, pl.ds(0, width // 2)] = pair_coords(cen, rad, units)
            coefs = lift(two)
            cen, rad = merge_shapes(cen, rad)
            width //= 2
            level += 1
        return coefs[0], packed_shape(cen[0], rad[0])

    sub_levels, leaf_levels = ns.bit_length() - 1, nl.bit_length() - 1
    for copy in sub_copies:
        copy.wait()
    top_coef, top_shape = climb(got_sub[...], ns, 0, sub_id)
    root_b[0:R, :] = top_coef
    root_b[R : R + 8, :] = top_shape
    leaf_copies = [
        send(root_b, got_leaf.at[leaf_id], leaf_send.at[o], leaf_recv.at[o], device)
        for o, device in enumerate(leaf_devs)
    ]
    got_leaf[leaf_id] = root_b[...]

    for copy in coup_copies:
        copy.wait()
    middle_row = lax.broadcasted_iota(jnp.int32, (1, 8, 128), 1)
    middle = jnp.where(
        middle_row == 2,
        (me * GROUPS + GROUPS // 2).astype(F32),
        jnp.where(middle_row < 2, 1.0, 0.0),
    )

    def put_leaves(where, cen, rad):
        u, v = features(SCALE * (cen - middle + rad * units[None]), 1)
        lower = lower_lanes(v.shape)
        v_left[pl.ds(where, 8)] = jnp.where(lower, v, 0.0).astype(BF16)
        v_right[pl.ds(where, 8)] = jnp.where(lower, 0.0, v).astype(BF16)
        return u

    def put_coefs(where, two):
        lower = lower_lanes((R, 128))
        first_left = jnp.where(lower, two, 0.0)
        second_right = jnp.where(lower, 0.0, two)
        c_left[where] = first_left.astype(BF16)
        c_right[where] = pltpu.roll(first_left, K, 1).astype(BF16)
        c_left[where + 1] = pltpu.roll(second_right, K, 1).astype(BF16)
        c_right[where + 1] = second_right.astype(BF16)

    @pl.loop(0, LD // 8)
    def _(b):
        u = put_leaves(REACH + b * 8, centers[pl.ds(b * 8, 8)], radii[pl.ds(b * 8, 8)])
        up_pair[pl.ds(b * 4, 4)] = side_by_side(u).astype(BF16)
        for s in range(4):
            put_coefs(REACH + b * 8 + 2 * s, pairs[b * 4 + s])

    for side, start, lane0 in ((0, 0, REACH), (1, REACH + LD, 0)):
        shape = halo_shape[side]
        for b in range(REACH // 8):
            cens, rads = [], []
            for s in range(8):
                lane = lane0 + b * 8 + s
                column = jnp.broadcast_to(shape[:, lane : lane + 1], (8, 128))
                cens.append(jnp.where(row8 < 3, column, 0.0))
                rads.append(jnp.broadcast_to(column[3:4, :], (8, 128)))
            put_leaves(start + b * 8, jnp.stack(cens), jnp.stack(rads))

        @pl.loop(0, REACH // 16)
        def _(b):
            for s in range(8):
                put_coefs(start + b * 16 + 2 * s, halo_coef[side, b * 8 + s].astype(F32))

    dead = LD + 2 * REACH
    for ref in (c_left, c_right, v_left, v_right):
        ref[dead] = jnp.zeros(ref.shape[1:], BF16)

    @pl.loop(0, LD // 2)
    def _(m):
        u = jnp.transpose(up_pair[m].astype(F32)).astype(BF16)
        tiles, sources = [], []
        for s in range(2):
            leaf = 2 * m + s
            vs, cs = [], []
            for t in range(4):
                picked = []
                for slot in (2 * t, 2 * t + 1):
                    j = coupling_list[leaf, slot]
                    near_by = jnp.clip(j - first + REACH, 0, dead - 1)
                    picked.append(jnp.where(j >= 0, near_by, dead))
                vs.append(v_left[picked[0]] + v_right[picked[1]])
                cs.append(c_left[picked[0]] + c_right[picked[1]])
            d2 = dot(u[s * K : (s + 1) * K], jnp.concatenate(vs, axis=1))
            tiles.append(from_square(d2).astype(BF16))
            sources.append(jnp.concatenate(cs, axis=1))
        product = dot_nt(jnp.concatenate(sources, axis=0), jnp.concatenate(tiles, axis=0))
        lc[m] = jnp.where(lane_half, product[:R], product[R:])

    for copy in leaf_copies:
        copy.wait()
    climb(got_leaf[...], nl, sub_levels, leaf_id)

    def masked(pair, side):
        chosen = lower_lanes(pair.shape) == (side == 0)
        return jnp.where(chosen, pair, 0.0)

    held = None
    for level in reversed(range(sub_levels + leaf_levels)):
        position = (sub_id if level < sub_levels else leaf_id)
        shift = level if level < sub_levels else level - sub_levels
        node = position // (2**shift)
        pair = node // 2
        mine = couple_pair(path_pair[level, pair], path_co[level, pair])
        if held is not None:
            mine = mine + dot3(held, down_high, down_low)
        held = masked(mine, lax.rem(node, 2))

    def spread(pair_block):
        n = pair_block.shape[0]
        lower = lower_lanes(pair_block.shape)
        both = jnp.stack(
            [jnp.where(lower, pair_block, 0.0), jnp.where(lower, 0.0, pair_block)], axis=1
        )
        return dot3(both.reshape(2 * n * R, 128), down_high, down_low).reshape(2 * n, R, 128)

    n, offset = 1, LD // 2 - 2
    block = sib[pl.ds(offset, 1)] + dot3(held, down_high, down_low)[None]
    while n < LD // 4:
        block = spread(block)
        n *= 2
        offset -= n
        block = block + sib[pl.ds(offset, n)]
    e0[...] = spread(block)

    @pl.loop(0, LD // 16)
    def _(b):
        for s in range(8):
            m = b * 8 + s
            coef = lc[m] + e0[m]
            stacked = jnp.concatenate(
                [jnp.where(lane_half, coef, 0.0), jnp.where(lane_half, 0.0, coef)], axis=0
            ).astype(BF16)
            far = dot(stacked, basis[pl.ds(2 * m, 2)].reshape(2 * K, PT))
            start = pl.multiple_of(m * 256, 256)
            near = oe[:, pl.ds(pl.multiple_of(GW + m * 256, 256), 256)]
            out[:, pl.ds(start, 256)] = near + jnp.concatenate([far[:R], far[R:]], axis=1)


def per_device(charges, points, basis, transfer, near_list, coupling_list):
    nl, ns = lax.axis_size("leaf"), lax.axis_size("sub")
    levels = (nl * ns).bit_length() - 1
    widest = max(nl, ns) // 2
    vmem = pl.BlockSpec(memory_space=pltpu.VMEM)
    total = LD + 2 * REACH + 1

    def body(*refs):
        kernel(nl, ns, *refs)

    dma = pltpu.SemaphoreType.DMA
    return pl.pallas_call(
        body,
        out_shape=jax.ShapeDtypeStruct((R, LD * PT), F32),
        in_specs=[vmem] * 5 + [pl.BlockSpec(memory_space=pltpu.SMEM)],
        out_specs=vmem,
        scratch_shapes=[
            pltpu.VMEM((8, EXT), F32),
            pltpu.VMEM((R, EXT), BF16),
            pltpu.VMEM((R, EXT), F32),
            pltpu.VMEM((FEAT, EXT), BF16),
            pltpu.VMEM((FEAT, EXT), BF16),
            pltpu.VMEM((FEAT, EXT), BF16),
            pltpu.VMEM((3 * GRP, LD + 2 * GRP, 128), F32),
            pltpu.VMEM((LD, 8, 128), F32),
            pltpu.VMEM((LD, 8, 128), F32),
            pltpu.VMEM((LD, 8, 128), F32),
            pltpu.VMEM((LD, R, 128), F32),
            pltpu.VMEM((LD // 2, 8, 128), F32),
            pltpu.VMEM((LD // 2, R, 128), F32),
            pltpu.VMEM((LD // 2, FEAT, 128), BF16),
            pltpu.VMEM((total, FEAT, 128), BF16),
            pltpu.VMEM((total, FEAT, 128), BF16),
            pltpu.VMEM((total, R, 128), BF16),
            pltpu.VMEM((total, R, 128), BF16),
            pltpu.VMEM((LD // 2, R, 128), F32),
            pltpu.VMEM((LD // 2, R, 128), BF16),
            pltpu.VMEM((2, REACH // 2, R, 128), BF16),
            pltpu.VMEM((8, 128), F32),
            pltpu.VMEM((2, 8, 128), F32),
            pltpu.VMEM((R + 8, 128), F32),
            pltpu.VMEM((ns, R + 8, 128), F32),
            pltpu.VMEM((R + 8, 128), F32),
            pltpu.VMEM((nl, R + 8, 128), F32),
            pltpu.VMEM((levels, widest, R, 128), F32),
            pltpu.VMEM((levels, widest, 8, 128), F32),
            pltpu.VMEM((LD // 2, R, 128), F32),
            dma((4,)), dma((4,)), dma((4,)), dma((4,)),
            dma((ns,)), dma((ns,)), dma((nl,)), dma((nl,)),
        ],
        compiler_params=pltpu.CompilerParams(
            collective_id=0, has_side_effects=True, vmem_limit_bytes=56 * 2**20
        ),
        cost_estimate=pl.CostEstimate(
            flops=6 * 10**9, bytes_accessed=7 * 10**6, transcendentals=4 * 10**7
        ),
    )(charges, points, basis, transfer, near_list, coupling_list)


def solution(mesh):
    in_specs = (
        P(None, ("leaf", "sub")),
        P(None, ("leaf", "sub")),
        P(("leaf", "sub"), None, None),
        P(),
        P(("leaf", "sub"), None),
        P(("leaf", "sub"), None),
    )
    return jax.shard_map(
        per_device,
        mesh=mesh,
        in_specs=in_specs,
        out_specs=P(None, ("leaf", "sub")),
        check_vma=False,
    )
```

```python
import math

import jax
import jax.numpy as jnp
from jax import lax
from jax.experimental import pallas as pl
from jax.experimental.pallas import tpu as pltpu
from jax.sharding import PartitionSpec as P

F32, BF16 = jnp.float32, jnp.bfloat16
PT = 128
K = 64
R = 32
LD = 128
REACH = 64
GRP = 4
GW = GRP * PT
GROUPS = LD // GRP
EXT = (GROUPS + 2) * GW
FEAT = 48
SCALE = math.log2(math.e) / 2.0
TINY = 1e-30
MESH = pl.DeviceIdType.MESH


def dot(a, b):
    return lax.dot_general(a, b, (((1,), (0,)), ((), ())), preferred_element_type=F32)


def dot_nt(a, b):
    return lax.dot_general(a, b, (((1,), (1,)), ((), ())), preferred_element_type=F32)


def dot_tn(a, b):
    return lax.dot_general(a, b, (((0,), (0,)), ((), ())), preferred_element_type=F32)


def split2(x):
    high = x.astype(BF16)
    return high, (x - high.astype(F32)).astype(BF16)


def dot3(a, b_high, b_low):
    high, low = split2(a)
    n = a.shape[0]
    both = dot(jnp.concatenate([high, low], axis=0), b_high)
    return both[:n] + (dot(high, b_low) + both[n:])


def from_square(d2):
    x = jnp.maximum(d2, TINY)
    return jnp.exp2(-(x * lax.rsqrt(x)))


def features(coords, axis):
    high = coords.astype(BF16).astype(F32)
    low = (coords - high).astype(BF16).astype(F32)
    kept = high + low
    norm = jnp.sum(kept * kept, axis=axis, keepdims=True)
    n1 = norm.astype(BF16).astype(F32)
    n2 = (norm - n1).astype(BF16).astype(F32)
    n3 = norm - n1 - n2
    row = lax.broadcasted_iota(jnp.int32, coords.shape, axis)
    norms = jnp.where(row == 0, n1, jnp.where(row == 1, n2, jnp.where(row == 2, n3, 0.0)))
    ones = jnp.where(row < 3, 1.0, 0.0)
    high2, low2 = -2.0 * high, -2.0 * low
    u = jnp.concatenate([high, high, low, low, norms, ones], axis=axis)
    v = jnp.concatenate([high2, low2, high2, low2, ones, norms], axis=axis)
    return u, v


def unit_rows():
    row = lax.broadcasted_iota(jnp.int32, (8, 128), 0)
    index = lax.broadcasted_iota(jnp.int32, (8, 128), 1) % K
    digit = jnp.where(row == 0, index // 16, jnp.where(row == 1, index // 4 % 4, index % 4))
    big, small = math.cos(math.pi / 8.0), math.cos(3.0 * math.pi / 8.0)
    value = jnp.where(
        digit == 0, big, jnp.where(digit == 1, small, jnp.where(digit == 2, -small, -big))
    )
    return jnp.where(row < 3, value, 0.0).astype(F32)


def lower_lanes(shape):
    return lax.broadcasted_iota(jnp.int32, shape, len(shape) - 1) < K


def halves(x):
    paired = x.reshape((x.shape[0] // 2, 2) + x.shape[1:])
    return paired[:, 0], paired[:, 1]


def side_by_side(x):
    left, right = halves(x)
    return jnp.where(lower_lanes(left.shape), left, right)


def merge_shapes(centers, radii):
    c0, c1 = halves(centers)
    r0, r1 = halves(radii)
    gap = c0 - c1
    reach = jnp.sqrt(jnp.sum(gap * gap, axis=1, keepdims=True))
    return 0.5 * (c0 + c1), jnp.maximum(r0, r1) + 0.5 * reach


def pair_coords(centers, radii, units):
    c0, c1 = halves(centers)
    r0, r1 = halves(radii)
    half = 0.5 * (c0 - c1)
    left = lower_lanes(half.shape)
    return SCALE * (jnp.where(left, half, -half) + jnp.where(left, r0, r1) * units[None])


def couple_square(coefs, d2):
    across = (lax.broadcasted_iota(jnp.int32, (128, 128), 0) < K) != lower_lanes((128, 128))
    tile = jnp.where(across, from_square(d2), 0.0)
    tile_high, tile_low = split2(tile)
    return dot3(coefs, tile_high, tile_low)


def block_diagonal(x):
    leaf = lax.broadcasted_iota(jnp.int32, x.shape, 1) // PT
    wide = x.astype(F32)
    return jnp.concatenate(
        [jnp.where(leaf == k, wide, 0.0) for k in range(GRP)], axis=0
    ).astype(BF16)


def couple_pair(coefs, coords):
    columns = jnp.transpose(coords)
    d2 = None
    for k in range(3):
        gap = columns[:, k : k + 1] - coords[k : k + 1, :]
        d2 = gap * gap if d2 is None else d2 + gap * gap
    return couple_square(coefs, d2)


def kernel(
    nl, ns,
    charges, points, basis, transfer, near_list, coupling_list,
    out,
    p8, xe, oe, ua, va, vb, xd, inner0, cross0, inner1, cross1, weight,
    leaf_pts, centers, radii, pairs, pair_co, sib,
    up_pair, v_left, v_right, c_left, c_right, lc,
    send_coef, halo_coef, send_shape, halo_shape,
    root, got_sub, root_b, got_leaf, path_pair, path_co, e0,
    near_send, near_recv, coup_send, coup_recv, sub_send, sub_recv, leaf_send, leaf_recv,
):
    leaf_id, sub_id = lax.axis_index("leaf"), lax.axis_index("sub")
    count = nl * ns
    me = leaf_id * ns + sub_id
    right, left = lax.rem(me + 1, count), lax.rem(me + count - 1, count)
    left_dev = (left // ns, lax.rem(left, ns))
    right_dev = (right // ns, lax.rem(right, ns))
    sub_devs = [(leaf_id, lax.rem(sub_id + o, ns)) for o in range(1, ns)]
    leaf_devs = [(lax.rem(leaf_id + o, nl), sub_id) for o in range(1, nl)]
    barrier = pltpu.get_barrier_semaphore()
    partners = [left_dev, right_dev] + sub_devs + leaf_devs
    for device in partners:
        pl.semaphore_signal(barrier, inc=1, device_id=device, device_id_type=MESH)

    def send(src, dst, send_sem, recv_sem, device):
        copy = pltpu.make_async_remote_copy(
            src_ref=src, dst_ref=dst, send_sem=send_sem, recv_sem=recv_sem,
            device_id=device, device_id_type=MESH,
        )
        copy.start()
        return copy

    first = me * LD
    units = unit_rows()
    lane_half = lower_lanes((R, 128))

    p8[3:8, GW : EXT - GW] = jnp.zeros((5, LD * PT), F32)
    p8[0:3, GW : EXT - GW] = points[...]

    pl.semaphore_wait(barrier, len(partners))
    copies = []
    copies.append(send(charges.at[:, pl.ds(0, GW)], xe.at[:, pl.ds(EXT - GW, GW)],
                       near_send.at[0], near_recv.at[0], left_dev))
    copies.append(send(charges.at[:, pl.ds(LD * PT - GW, GW)], xe.at[:, pl.ds(0, GW)],
                       near_send.at[1], near_recv.at[1], right_dev))
    copies.append(send(p8.at[:, pl.ds(GW, GW)], p8.at[:, pl.ds(EXT - GW, GW)],
                       near_send.at[2], near_recv.at[2], left_dev))
    copies.append(send(p8.at[:, pl.ds(EXT - 2 * GW, GW)], p8.at[:, pl.ds(0, GW)],
                       near_send.at[3], near_recv.at[3], right_dev))
    near_copies = copies

    for c in range(LD):
        leaf_pts[c] = p8[:, GW + c * PT : GW + (c + 1) * PT]

    @pl.loop(0, LD // 16)
    def _(block):
        rows = pl.ds(block * 16, 16)
        pts = leaf_pts[rows]
        center = jnp.mean(pts, axis=2, keepdims=True)
        off = pts - center
        far = jnp.max(jnp.sum(off * off, axis=1, keepdims=True), axis=2, keepdims=True)
        centers[rows] = jnp.broadcast_to(center, pts.shape)
        radii[rows] = jnp.broadcast_to(jnp.sqrt(far), pts.shape)

    row8 = lax.broadcasted_iota(jnp.int32, (8, 128), 0)
    lane8 = lax.broadcasted_iota(jnp.int32, (8, 128), 1)

    packed = jnp.zeros((8, 128), F32)
    for c in range(LD):
        packed = jnp.where(lane8 == c, jnp.where(row8 < 3, centers[c], radii[c]), packed)
    send_shape[...] = packed

    @pl.loop(0, LD // 16)
    def _(block):
        for s in range(8):
            m = block * 8 + s
            x = charges[:, pl.ds(pl.multiple_of(m * 256, 256), 256)]
            stacked = jnp.concatenate([x[:, :128], x[:, 128:]], axis=0)
            both = basis[pl.ds(2 * m, 2)].reshape(2 * K, PT)
            product = dot_nt(stacked, both)
            pair = jnp.where(lane_half, product[:R], product[R:])
            pairs[m] = pair
            send_coef[m] = pair.astype(BF16)

    half_pairs = REACH // 2
    coup_copies = [
        send(send_coef.at[pl.ds(0, half_pairs)], halo_coef.at[1],
             coup_send.at[0], coup_recv.at[0], left_dev),
        send(send_coef.at[pl.ds(half_pairs, half_pairs)], halo_coef.at[0],
             coup_send.at[1], coup_recv.at[1], right_dev),
        send(send_shape, halo_shape.at[1], coup_send.at[2], coup_recv.at[2], left_dev),
        send(send_shape, halo_shape.at[0], coup_send.at[3], coup_recv.at[3], right_dev),
    ]

    t0, t1 = transfer[0], transfer[1]
    up = jnp.concatenate([t0, t1], axis=0)
    up_high, up_low = split2(jnp.concatenate([up, up], axis=1))
    down = jnp.concatenate([jnp.transpose(t0), jnp.transpose(t1)], axis=1)
    down_high, down_low = split2(jnp.concatenate([down, down], axis=0))

    def lift(pair_block):
        n = pair_block.shape[0]
        return dot3(pair_block.reshape(n * R, 128), up_high, up_low).reshape(n, R, 128)

    level_cen, level_rad = centers[...], radii[...]
    offset, n = 0, LD // 2
    block = pairs[pl.ds(0, n)]
    while n > 1:
        block = side_by_side(lift(block))
        level_cen, level_rad = merge_shapes(level_cen, level_rad)
        offset += n
        n //= 2
        pairs[pl.ds(offset, n)] = block
        pair_co[pl.ds(offset - LD // 2, n)] = pair_coords(level_cen, level_rad, units)
    root_coef = lift(block)[0]
    root_cen, root_rad = merge_shapes(level_cen, level_rad)

    def packed_shape(cen, rad):
        return jnp.where(row8 < 3, cen, rad)

    def unpacked_shape(shape):
        rows = lax.broadcasted_iota(jnp.int32, shape.shape, 1)
        cen = jnp.where(rows < 3, shape, 0.0)
        rad = jnp.sum(jnp.where(rows == 3, shape, 0.0), axis=1, keepdims=True)
        return cen, jnp.broadcast_to(rad, shape.shape)

    root[0:R, :] = root_coef
    root[R : R + 8, :] = packed_shape(root_cen[0], root_rad[0])
    sub_copies = [
        send(root, got_sub.at[sub_id], sub_send.at[o], sub_recv.at[o], device)
        for o, device in enumerate(sub_devs)
    ]
    got_sub[sub_id] = root[...]

    @pl.loop(0, 9)
    def _(i):
        for s in range(7):
            u, v = features(pair_co[i * 7 + s], 0)
            d2 = dot_tn(u.astype(BF16), v.astype(BF16))
            sib[i * 7 + s] = couple_square(pairs[LD // 2 + i * 7 + s], d2)

    xe[:, GW : EXT - GW] = charges[...]
    oe[:, GW : EXT - GW] = charges[...].astype(F32)
    leaf_row = lax.broadcasted_iota(jnp.int32, (LD, 1), 0)
    base = first + (leaf_row // GRP) * GRP - GRP
    listed = jnp.transpose(near_list[...])
    relative = jnp.where(listed >= 0, listed - base, -1)
    weight[...] = jnp.zeros_like(weight)
    for k in range(3 * GRP):
        times = jnp.sum(jnp.where(relative == k, 1.0, 0.0), axis=1, keepdims=True)
        weight[k, GRP : GRP + LD, :] = jnp.broadcast_to(times, (LD, 128))

    for copy in near_copies:
        copy.wait()

    @pl.loop(0, GROUPS + 2)
    def _(g):
        lanes = pl.ds(pl.multiple_of(g * GW, GW), GW)
        row = lax.broadcasted_iota(jnp.int32, (8, GW), 0)
        z0 = (me * GROUPS + g - 1).astype(F32)
        corner = jnp.where(row == 2, z0, jnp.where(row < 2, 1.0, 0.0))
        low = p8[:, lanes] - corner
        shift = jnp.where(row == 2, 1.0, 0.0)
        u, v = features(SCALE * (low - shift), 0)
        ua[:, lanes] = u.astype(BF16)
        va[:, lanes] = v.astype(BF16)
        vb[:, lanes] = features(SCALE * low, 0)[1].astype(BF16)
        xd[pl.ds(pl.multiple_of(g * 128, 128), 128), :] = block_diagonal(xe[:, lanes])

    oe[:, 0:GW] = jnp.zeros((R, GW), F32)
    oe[:, EXT - GW : EXT] = jnp.zeros((R, GW), F32)

    def near_tiles(g, inner, cross):
        here = pl.ds(pl.multiple_of(g * GW, GW), GW)
        there = pl.ds(pl.multiple_of(g * GW + GW, GW), GW)
        u, v, v_next = ua[:, here], va[:, here], vb[:, there]
        for i in range(GRP):
            rows = slice(i * PT, (i + 1) * PT)
            inner[rows, i * PT :] = from_square(dot_tn(u[:, rows], v[:, i * PT :])).astype(BF16)
            cross[rows, :] = from_square(dot_tn(u[:, rows], v_next)).astype(BF16)

    def near_sums(g, inner, cross):
        here = pl.ds(pl.multiple_of(g * GW, GW), GW)
        there = pl.ds(pl.multiple_of(g * GW + GW, GW), GW)

        def times(k, target):
            return weight[k, pl.ds(g * GRP + target, 1), :]

        def part(block, source, target=0):
            return block[source * R : (source + 1) * R, target * PT : (target + 1) * PT]

        x = xd[pl.ds(pl.multiple_of(g * 128, 128), 128), :]
        x_next = xd[pl.ds(pl.multiple_of(g * 128 + 128, 128), 128), :]
        own = [part(oe[:, here], 0, j) for j in range(GRP)]
        following = [part(oe[:, there], 0, j) for j in range(GRP)]
        for j in range(GRP):
            n = j + 1
            to_later = dot(x[: n * R, : n * PT], inner[: n * PT, j * PT : (j + 1) * PT])
            for i in range(n):
                own[j] = own[j] + times(GRP + i, j) * part(to_later, i)
        for i in range(GRP - 1):
            n = i + 1
            to_earlier = dot_nt(x[n * R :, n * PT :], inner[i * PT : n * PT, n * PT :])
            for j in range(n, GRP):
                own[i] = own[i] + times(GRP + j, i) * part(to_earlier, j - n)
        forth, back = dot(x, cross[...]), dot_nt(x_next, cross[...])
        for j in range(GRP):
            for i in range(GRP):
                following[j] = following[j] + times(i, GRP + j) * part(forth, i, j)
                own[i] = own[i] + times(2 * GRP + j, i) * part(back, j, i)
        oe[:, here] = jnp.concatenate(own, axis=1)
        oe[:, there] = jnp.concatenate(following, axis=1)

    near_tiles(0, inner0, cross0)

    @pl.loop(0, GROUPS // 2)
    def _(h):
        near_tiles(2 * h + 1, inner1, cross1)
        near_sums(2 * h, inner0, cross0)
        near_tiles(2 * h + 2, inner0, cross0)
        near_sums(2 * h + 1, inner1, cross1)

    near_sums(GROUPS, inner0, cross0)

    def climb(got, width, level0, index):
        coefs = got[:, 0:R, :]
        cen, rad = unpacked_shape(got[:, R : R + 8, :])
        level = level0
        while width > 1:
            two = side_by_side(coefs)
            path_pair[level, pl.ds(0, width // 2)] = two
            path_co[level, pl.ds(0, width // 2)] = pair_coords(cen, rad, units)
            coefs = lift(two)
            cen, rad = merge_shapes(cen, rad)
            width //= 2
            level += 1
        return coefs[0], packed_shape(cen[0], rad[0])

    sub_levels, leaf_levels = ns.bit_length() - 1, nl.bit_length() - 1
    for copy in sub_copies:
        copy.wait()
    top_coef, top_shape = climb(got_sub[...], ns, 0, sub_id)
    root_b[0:R, :] = top_coef
    root_b[R : R + 8, :] = top_shape
    leaf_copies = [
        send(root_b, got_leaf.at[leaf_id], leaf_send.at[o], leaf_recv.at[o], device)
        for o, device in enumerate(leaf_devs)
    ]
    got_leaf[leaf_id] = root_b[...]

    for copy in coup_copies:
        copy.wait()
    middle_row = lax.broadcasted_iota(jnp.int32, (1, 8, 128), 1)
    middle = jnp.where(
        middle_row == 2,
        (me * GROUPS + GROUPS // 2).astype(F32),
        jnp.where(middle_row < 2, 1.0, 0.0),
    )

    def put_leaves(where, cen, rad):
        u, v = features(SCALE * (cen - middle + rad * units[None]), 1)
        lower = lower_lanes(v.shape)
        v_left[pl.ds(where, 8)] = jnp.where(lower, v, 0.0).astype(BF16)
        v_right[pl.ds(where, 8)] = jnp.where(lower, 0.0, v).astype(BF16)
        return u

    def put_coefs(where, two):
        lower = lower_lanes((R, 128))
        first_left = jnp.where(lower, two, 0.0)
        second_right = jnp.where(lower, 0.0, two)
        c_left[where] = first_left.astype(BF16)
        c_right[where] = pltpu.roll(first_left, K, 1).astype(BF16)
        c_left[where + 1] = pltpu.roll(second_right, K, 1).astype(BF16)
        c_right[where + 1] = second_right.astype(BF16)

    @pl.loop(0, LD // 8)
    def _(b):
        u = put_leaves(REACH + b * 8, centers[pl.ds(b * 8, 8)], radii[pl.ds(b * 8, 8)])
        up_pair[pl.ds(b * 4, 4)] = side_by_side(u).astype(BF16)
        for s in range(4):
            put_coefs(REACH + b * 8 + 2 * s, pairs[b * 4 + s])

    for side, start, lane0 in ((0, 0, REACH), (1, REACH + LD, 0)):
        shape = halo_shape[side]
        for b in range(REACH // 8):
            cens, rads = [], []
            for s in range(8):
                lane = lane0 + b * 8 + s
                column = jnp.broadcast_to(shape[:, lane : lane + 1], (8, 128))
                cens.append(jnp.where(row8 < 3, column, 0.0))
                rads.append(jnp.broadcast_to(column[3:4, :], (8, 128)))
            put_leaves(start + b * 8, jnp.stack(cens), jnp.stack(rads))

        @pl.loop(0, REACH // 16)
        def _(b):
            for s in range(8):
                put_coefs(start + b * 16 + 2 * s, halo_coef[side, b * 8 + s].astype(F32))

    dead = LD + 2 * REACH
    for ref in (c_left, c_right, v_left, v_right):
        ref[dead] = jnp.zeros(ref.shape[1:], BF16)

    def listed(m):
        u = jnp.transpose(up_pair[m].astype(F32)).astype(BF16)
        tiles, sources = [], []
        for s in range(2):
            leaf = 2 * m + s
            vs, cs = [], []
            for t in range(4):
                picked = []
                for slot in (2 * t, 2 * t + 1):
                    j = coupling_list[slot, leaf]
                    near_by = jnp.clip(j - first + REACH, 0, dead - 1)
                    picked.append(jnp.where(j >= 0, near_by, dead))
                vs.append(v_left[picked[0]] + v_right[picked[1]])
                cs.append(c_left[picked[0]] + c_right[picked[1]])
            d2 = dot(u[s * K : (s + 1) * K], jnp.concatenate(vs, axis=1))
            tiles.append(from_square(d2).astype(BF16))
            sources.append(jnp.concatenate(cs, axis=1))
        return jnp.concatenate(sources, axis=0), jnp.concatenate(tiles, axis=0)

    @pl.loop(0, LD // 8)
    def _(b):
        operands = [listed(b * 4 + s) for s in range(4)]
        for s in range(4):
            product = dot_nt(*operands[s])
            lc[b * 4 + s] = jnp.where(lane_half, product[:R], product[R:])

    for copy in leaf_copies:
        copy.wait()
    climb(got_leaf[...], nl, sub_levels, leaf_id)

    def masked(pair, side):
        chosen = lower_lanes(pair.shape) == (side == 0)
        return jnp.where(chosen, pair, 0.0)

    held = None
    for level in reversed(range(sub_levels + leaf_levels)):
        position = (sub_id if level < sub_levels else leaf_id)
        shift = level if level < sub_levels else level - sub_levels
        node = position // (2**shift)
        pair = node // 2
        mine = couple_pair(path_pair[level, pair], path_co[level, pair])
        if held is not None:
            mine = mine + dot3(held, down_high, down_low)
        held = masked(mine, lax.rem(node, 2))

    def spread(pair_block):
        n = pair_block.shape[0]
        lower = lower_lanes(pair_block.shape)
        both = jnp.stack(
            [jnp.where(lower, pair_block, 0.0), jnp.where(lower, 0.0, pair_block)], axis=1
        )
        return dot3(both.reshape(2 * n * R, 128), down_high, down_low).reshape(2 * n, R, 128)

    n, offset = 1, LD // 2 - 2
    block = sib[pl.ds(offset, 1)] + dot3(held, down_high, down_low)[None]
    while n < LD // 4:
        block = spread(block)
        n *= 2
        offset -= n
        block = block + sib[pl.ds(offset, n)]
    e0[...] = spread(block)

    @pl.loop(0, LD // 16)
    def _(b):
        for s in range(8):
            m = b * 8 + s
            coef = lc[m] + e0[m]
            stacked = jnp.concatenate(
                [jnp.where(lane_half, coef, 0.0), jnp.where(lane_half, 0.0, coef)], axis=0
            ).astype(BF16)
            far = dot(stacked, basis[pl.ds(2 * m, 2)].reshape(2 * K, PT))
            start = pl.multiple_of(m * 256, 256)
            near = oe[:, pl.ds(pl.multiple_of(GW + m * 256, 256), 256)]
            out[:, pl.ds(start, 256)] = near + jnp.concatenate([far[:R], far[R:]], axis=1)


def per_device(charges, points, basis, transfer, near_list, coupling_list):
    nl, ns = lax.axis_size("leaf"), lax.axis_size("sub")
    levels = (nl * ns).bit_length() - 1
    widest = max(nl, ns) // 2
    vmem = pl.BlockSpec(memory_space=pltpu.VMEM)
    total = LD + 2 * REACH + 1

    def body(*refs):
        kernel(nl, ns, *refs)

    dma = pltpu.SemaphoreType.DMA
    return pl.pallas_call(
        body,
        out_shape=jax.ShapeDtypeStruct((R, LD * PT), F32),
        in_specs=[vmem] * 5 + [pl.BlockSpec(memory_space=pltpu.SMEM)],
        out_specs=vmem,
        scratch_shapes=[
            pltpu.VMEM((8, EXT), F32),
            pltpu.VMEM((R, EXT), BF16),
            pltpu.VMEM((R, EXT), F32),
            pltpu.VMEM((FEAT, EXT), BF16),
            pltpu.VMEM((FEAT, EXT), BF16),
            pltpu.VMEM((FEAT, EXT), BF16),
            pltpu.VMEM(((GROUPS + 2) * 128, GW), BF16),
            pltpu.VMEM((GW, GW), BF16),
            pltpu.VMEM((GW, GW), BF16),
            pltpu.VMEM((GW, GW), BF16),
            pltpu.VMEM((GW, GW), BF16),
            pltpu.VMEM((3 * GRP, LD + 2 * GRP, 128), F32),
            pltpu.VMEM((LD, 8, 128), F32),
            pltpu.VMEM((LD, 8, 128), F32),
            pltpu.VMEM((LD, 8, 128), F32),
            pltpu.VMEM((LD, R, 128), F32),
            pltpu.VMEM((LD // 2, 8, 128), F32),
            pltpu.VMEM((LD // 2, R, 128), F32),
            pltpu.VMEM((LD // 2, FEAT, 128), BF16),
            pltpu.VMEM((total, FEAT, 128), BF16),
            pltpu.VMEM((total, FEAT, 128), BF16),
            pltpu.VMEM((total, R, 128), BF16),
            pltpu.VMEM((total, R, 128), BF16),
            pltpu.VMEM((LD // 2, R, 128), F32),
            pltpu.VMEM((LD // 2, R, 128), BF16),
            pltpu.VMEM((2, REACH // 2, R, 128), BF16),
            pltpu.VMEM((8, 128), F32),
            pltpu.VMEM((2, 8, 128), F32),
            pltpu.VMEM((R + 8, 128), F32),
            pltpu.VMEM((ns, R + 8, 128), F32),
            pltpu.VMEM((R + 8, 128), F32),
            pltpu.VMEM((nl, R + 8, 128), F32),
            pltpu.VMEM((levels, widest, R, 128), F32),
            pltpu.VMEM((levels, widest, 8, 128), F32),
            pltpu.VMEM((LD // 2, R, 128), F32),
            dma((4,)), dma((4,)), dma((4,)), dma((4,)),
            dma((ns,)), dma((ns,)), dma((nl,)), dma((nl,)),
        ],
        compiler_params=pltpu.CompilerParams(
            collective_id=0, has_side_effects=True, vmem_limit_bytes=56 * 2**20
        ),
        cost_estimate=pl.CostEstimate(
            flops=6 * 10**9, bytes_accessed=7 * 10**6, transcendentals=4 * 10**7
        ),
    )(charges, points, basis, transfer, near_list.T, coupling_list.T)


def solution(mesh):
    in_specs = (
        P(None, ("leaf", "sub")),
        P(None, ("leaf", "sub")),
        P(("leaf", "sub"), None, None),
        P(),
        P(("leaf", "sub"), None),
        P(("leaf", "sub"), None),
    )
    return jax.shard_map(
        per_device,
        mesh=mesh,
        in_specs=in_specs,
        out_specs=P(None, ("leaf", "sub")),
        check_vma=False,
    )
```

```python
import math

import jax
import jax.numpy as jnp
from jax import lax
from jax.experimental import pallas as pl
from jax.experimental.pallas import tpu as pltpu
from jax.sharding import PartitionSpec as P

F32, BF16 = jnp.float32, jnp.bfloat16
PT = 128
K = 64
R = 32
LD = 128
REACH = 64
GRP = 4
GW = GRP * PT
GROUPS = LD // GRP
EXT = (GROUPS + 2) * GW
FEAT = 32
SCALE = math.log2(math.e) / 2.0
TINY = 1e-30
MESH = pl.DeviceIdType.MESH


def dot(a, b):
    return lax.dot_general(a, b, (((1,), (0,)), ((), ())), preferred_element_type=F32)


def dot_nt(a, b):
    return lax.dot_general(a, b, (((1,), (1,)), ((), ())), preferred_element_type=F32)


def dot_tn(a, b):
    return lax.dot_general(a, b, (((0,), (0,)), ((), ())), preferred_element_type=F32)


def split2(x):
    high = x.astype(BF16)
    return high, (x - high.astype(F32)).astype(BF16)


def dot3(a, b_high, b_low):
    high, low = split2(a)
    n = a.shape[0]
    both = dot(jnp.concatenate([high, low], axis=0), b_high)
    return both[:n] + (dot(high, b_low) + both[n:])


def from_square(d2):
    x = jnp.maximum(d2, TINY)
    return jnp.exp2(-(x * lax.rsqrt(x)))


def features(coords, axis):
    high = coords.astype(BF16).astype(F32)
    low = (coords - high).astype(BF16).astype(F32)
    kept = high + low
    norm = jnp.sum(kept * kept, axis=axis, keepdims=True)
    n1 = norm.astype(BF16).astype(F32)
    n2 = (norm - n1).astype(BF16).astype(F32)
    n3 = norm - n1 - n2
    row = lax.broadcasted_iota(jnp.int32, coords.shape, axis)
    ones = jnp.where((row >= 4) & (row < 7), 1.0, 0.0)
    norms = jnp.where(row == 0, n1, jnp.where(row == 1, n2, jnp.where(row == 2, n3, ones)))
    both = high + pltpu.roll(low, 4, axis)
    twice = -2.0 * both
    zero = jnp.zeros_like(both)
    u = jnp.concatenate([both, both, norms, zero], axis=axis)
    v = jnp.concatenate(
        [twice, pltpu.roll(twice, 4, axis), pltpu.roll(norms, 4, axis), zero], axis=axis
    )
    return u, v


def unit_rows():
    row = lax.broadcasted_iota(jnp.int32, (8, 128), 0)
    index = lax.broadcasted_iota(jnp.int32, (8, 128), 1) % K
    digit = jnp.where(row == 0, index // 16, jnp.where(row == 1, index // 4 % 4, index % 4))
    big, small = math.cos(math.pi / 8.0), math.cos(3.0 * math.pi / 8.0)
    value = jnp.where(
        digit == 0, big, jnp.where(digit == 1, small, jnp.where(digit == 2, -small, -big))
    )
    return jnp.where(row < 3, value, 0.0).astype(F32)


def lower_lanes(shape):
    return lax.broadcasted_iota(jnp.int32, shape, len(shape) - 1) < K


def halves(x):
    paired = x.reshape((x.shape[0] // 2, 2) + x.shape[1:])
    return paired[:, 0], paired[:, 1]


def side_by_side(x):
    left, right = halves(x)
    return jnp.where(lower_lanes(left.shape), left, right)


def merge_shapes(centers, radii):
    c0, c1 = halves(centers)
    r0, r1 = halves(radii)
    gap = c0 - c1
    reach = jnp.sqrt(jnp.sum(gap * gap, axis=1, keepdims=True))
    return 0.5 * (c0 + c1), jnp.maximum(r0, r1) + 0.5 * reach


def pair_coords(centers, radii, units):
    c0, c1 = halves(centers)
    r0, r1 = halves(radii)
    half = 0.5 * (c0 - c1)
    left = lower_lanes(half.shape)
    return SCALE * (jnp.where(left, half, -half) + jnp.where(left, r0, r1) * units[None])


def couple_square(coefs, d2):
    across = (lax.broadcasted_iota(jnp.int32, (128, 128), 0) < K) != lower_lanes((128, 128))
    tile = jnp.where(across, from_square(d2), 0.0)
    tile_high, tile_low = split2(tile)
    return dot3(coefs, tile_high, tile_low)


def couple_near_pair(coefs, coords):
    u, v = features(coords, 0)
    lower = lower_lanes(v.shape)
    v_two = jnp.concatenate([jnp.where(lower, v, 0.0), jnp.where(lower, 0.0, v)], axis=0)
    columns = jnp.transpose(u)
    u_two = jnp.concatenate([columns[K:], columns[:K]], axis=1)
    tile_high, tile_low = split2(from_square(dot(u_two.astype(BF16), v_two.astype(BF16))))
    swapped = pltpu.roll(coefs, K, 1)
    both = dot3(jnp.concatenate([swapped[:, :K], coefs[:, :K]], axis=0), tile_high, tile_low)
    return jnp.where(lower_lanes((R, 128)), both[:R], both[R:])


def block_diagonal(x):
    leaf = lax.broadcasted_iota(jnp.int32, x.shape, 1) // PT
    wide = x.astype(F32)
    return jnp.concatenate(
        [jnp.where(leaf == k, wide, 0.0) for k in range(GRP)], axis=0
    ).astype(BF16)


def couple_pair(coefs, coords):
    columns = jnp.transpose(coords)
    d2 = None
    for k in range(3):
        gap = columns[:, k : k + 1] - coords[k : k + 1, :]
        d2 = gap * gap if d2 is None else d2 + gap * gap
    return couple_square(coefs, d2)


def kernel(
    nl, ns,
    charges, points, basis, transfer, near_list, coupling_list,
    out,
    p8, xe, oe, ua, va, vb, xd, inner0, cross0, inner1, cross1, weight,
    centers, radii, pairs, pair_co, sib,
    up_pair, v_all, c_all, lc,
    send_coef, halo_coef, send_shape, halo_shape,
    root, got_sub, root_b, got_leaf, path_pair, path_co, d1,
    near_send, near_recv, coup_send, coup_recv, sub_send, sub_recv, leaf_send, leaf_recv, local_sem,
):
    leaf_id, sub_id = lax.axis_index("leaf"), lax.axis_index("sub")
    count = nl * ns
    me = leaf_id * ns + sub_id
    right, left = lax.rem(me + 1, count), lax.rem(me + count - 1, count)
    left_dev = (left // ns, lax.rem(left, ns))
    right_dev = (right // ns, lax.rem(right, ns))
    sub_devs = [(leaf_id, lax.rem(sub_id + o, ns)) for o in range(1, ns)]
    leaf_devs = [(lax.rem(leaf_id + o, nl), sub_id) for o in range(1, nl)]
    barrier = pltpu.get_barrier_semaphore()
    partners = [left_dev, right_dev] + sub_devs + leaf_devs
    for device in partners:
        pl.semaphore_signal(barrier, inc=1, device_id=device, device_id_type=MESH)

    def send(src, dst, send_sem, recv_sem, device):
        copy = pltpu.make_async_remote_copy(
            src_ref=src, dst_ref=dst, send_sem=send_sem, recv_sem=recv_sem,
            device_id=device, device_id_type=MESH,
        )
        copy.start()
        return copy

    own_charges = pltpu.make_async_copy(
        charges, xe.at[:, pl.ds(GW, LD * PT)], local_sem.at[0]
    )
    own_charges.start()
    first = me * LD
    units = unit_rows()
    lane_half = lower_lanes((R, 128))

    p8[3:8, GW : EXT - GW] = jnp.zeros((5, LD * PT), F32)
    p8[0:3, GW : EXT - GW] = points[...]

    pl.semaphore_wait(barrier, len(partners))
    copies = []
    copies.append(send(charges.at[:, pl.ds(0, GW)], xe.at[:, pl.ds(EXT - GW, GW)],
                       near_send.at[0], near_recv.at[0], left_dev))
    copies.append(send(charges.at[:, pl.ds(LD * PT - GW, GW)], xe.at[:, pl.ds(0, GW)],
                       near_send.at[1], near_recv.at[1], right_dev))
    copies.append(send(p8.at[:, pl.ds(GW, GW)], p8.at[:, pl.ds(EXT - GW, GW)],
                       near_send.at[2], near_recv.at[2], left_dev))
    copies.append(send(p8.at[:, pl.ds(EXT - 2 * GW, GW)], p8.at[:, pl.ds(0, GW)],
                       near_send.at[3], near_recv.at[3], right_dev))
    near_copies = copies

    @pl.loop(0, LD // 16)
    def _(block):
        start = pl.multiple_of(GW + block * (16 * PT), 16 * PT // 4)
        wide = p8[:, pl.ds(start, 16 * PT)]
        pts = jnp.stack([wide[:, c * PT : (c + 1) * PT] for c in range(16)])
        rows = pl.ds(block * 16, 16)
        center = jnp.mean(pts, axis=2, keepdims=True)
        off = pts - center
        far = jnp.max(jnp.sum(off * off, axis=1, keepdims=True), axis=2, keepdims=True)
        centers[rows] = jnp.broadcast_to(center, pts.shape)
        radii[rows] = jnp.broadcast_to(jnp.sqrt(far), pts.shape)

    row8 = lax.broadcasted_iota(jnp.int32, (8, 128), 0)
    lane8 = lax.broadcasted_iota(jnp.int32, (8, 128), 1)

    packed_cen, packed_rad = centers[0], radii[0]
    for c in range(1, LD):
        packed_cen = jnp.where(lane8 == c, centers[c], packed_cen)
        packed_rad = jnp.where(lane8 == c, radii[c], packed_rad)
    send_shape[0:8, :] = packed_cen
    send_shape[8:16, :] = packed_rad

    @pl.loop(0, LD // 16)
    def _(block):
        for s in range(8):
            m = block * 8 + s
            x = charges[:, pl.ds(pl.multiple_of(m * 256, 256), 256)]
            stacked = jnp.concatenate([x[:, :128], x[:, 128:]], axis=0)
            both = basis[pl.ds(2 * m, 2)].reshape(2 * K, PT)
            product = dot_nt(stacked, both)
            pair = jnp.where(lane_half, product[:R], product[R:])
            pairs[m] = pair
            send_coef[m] = pair.astype(BF16)

    half_pairs = REACH // 2
    coup_copies = [
        send(send_coef.at[pl.ds(0, half_pairs)], halo_coef.at[1],
             coup_send.at[0], coup_recv.at[0], left_dev),
        send(send_coef.at[pl.ds(half_pairs, half_pairs)], halo_coef.at[0],
             coup_send.at[1], coup_recv.at[1], right_dev),
        send(send_shape, halo_shape.at[1], coup_send.at[2], coup_recv.at[2], left_dev),
        send(send_shape, halo_shape.at[0], coup_send.at[3], coup_recv.at[3], right_dev),
    ]

    t0, t1 = transfer[0], transfer[1]
    up = jnp.concatenate([t0, t1], axis=0)
    up_high, up_low = split2(jnp.concatenate([up, up], axis=1))
    down = jnp.concatenate([jnp.transpose(t0), jnp.transpose(t1)], axis=1)
    down_high, down_low = split2(jnp.concatenate([down, down], axis=0))

    def lift(pair_block):
        n = pair_block.shape[0]
        return dot3(pair_block.reshape(n * R, 128), up_high, up_low).reshape(n, R, 128)

    level_cen, level_rad = centers[...], radii[...]
    offset, n = 0, LD // 2
    block = None
    while n > 1:
        level_cen, level_rad = merge_shapes(level_cen, level_rad)
        if n >= 32:

            def lift_part(i, offset=offset, n=n):
                eight = pairs[pl.ds(offset + i * 8, 8)]
                pairs[pl.ds(offset + n + i * 4, 4)] = side_by_side(lift(eight))

            pl.loop(0, n // 8)(lift_part)
        else:
            if block is None:
                block = pairs[pl.ds(offset, n)]
            block = side_by_side(lift(block))
            pairs[pl.ds(offset + n, n // 2)] = block
        offset += n
        n //= 2
        pair_co[pl.ds(offset - LD // 2, n)] = pair_coords(level_cen, level_rad, units)
    root_coef = lift(block)[0]
    root_cen, root_rad = merge_shapes(level_cen, level_rad)

    def packed_shape(cen, rad):
        return jnp.where(row8 < 3, cen, rad)

    def unpacked_shape(shape):
        rows = lax.broadcasted_iota(jnp.int32, shape.shape, 1)
        cen = jnp.where(rows < 3, shape, 0.0)
        rad = jnp.sum(jnp.where(rows == 3, shape, 0.0), axis=1, keepdims=True)
        return cen, jnp.broadcast_to(rad, shape.shape)

    root[0:R, :] = root_coef
    root[R : R + 8, :] = packed_shape(root_cen[0], root_rad[0])
    sub_copies = [
        send(root, got_sub.at[sub_id], sub_send.at[o], sub_recv.at[o], device)
        for o, device in enumerate(sub_devs)
    ]
    got_sub[sub_id] = root[...]

    leaf_lane = lax.broadcasted_iota(jnp.int32, (8, LD), 1)
    base = first + (leaf_lane // GRP) * GRP - GRP
    listed_leaf = near_list[...]
    relative = jnp.where(listed_leaf >= 0, listed_leaf - base, -1)
    slot_row = lax.broadcasted_iota(jnp.int32, (16, LD), 0)
    counts = jnp.zeros((16, LD), F32)
    for k in range(3 * GRP):
        times = jnp.sum(jnp.where(relative == k, 1.0, 0.0), axis=0, keepdims=True)
        counts = jnp.where(slot_row == k, times, counts)
    columns = jnp.transpose(counts).astype(BF16)
    for k in range(3 * GRP):
        ones = jnp.where(slot_row == k, 1.0, 0.0).astype(BF16)
        weight[k, 0:8, :] = jnp.zeros((8, 128), F32)
        weight[k, 8 : 8 + LD, :] = dot(columns, ones)
        weight[k, 8 + LD : 16 + LD, :] = jnp.zeros((8, 128), F32)

    own_charges.wait()
    for copy in near_copies:
        copy.wait()

    def near_features(g):
        lanes = pl.ds(pl.multiple_of(g * GW, GW), GW)
        row = lax.broadcasted_iota(jnp.int32, (8, GW), 0)
        z0 = lax.convert_element_type(me * GROUPS + g - 1, F32)
        corner = jnp.where(row == 2, z0, jnp.where(row < 2, 1.0, 0.0))
        low = p8[:, lanes] - corner
        shift = jnp.where(row == 2, 1.0, 0.0)
        u, v = features(SCALE * (low - shift), 0)
        ua[:, lanes] = u.astype(BF16)
        va[:, lanes] = v.astype(BF16)
        vb[:, lanes] = features(SCALE * low, 0)[1].astype(BF16)
        xd[pl.ds(pl.multiple_of(g * 128, 128), 128), :] = block_diagonal(xe[:, lanes])

    oe[:, 0:GW] = jnp.zeros((R, GW), F32)

    def near_tiles(g, inner, cross):
        here = pl.ds(pl.multiple_of(g * GW, GW), GW)
        there = pl.ds(pl.multiple_of(g * GW + GW, GW), GW)
        u, v, v_next = ua[:, here], va[:, here], vb[:, there]
        for i in range(GRP):
            rows = slice(i * PT, (i + 1) * PT)
            inner[rows, i * PT :] = from_square(dot_tn(u[:, rows], v[:, i * PT :])).astype(BF16)
            cross[rows, :] = from_square(dot_tn(u[:, rows], v_next)).astype(BF16)

    def near_sums(g, inner, cross):
        here = pl.ds(pl.multiple_of(g * GW, GW), GW)
        there = pl.ds(pl.multiple_of(g * GW + GW, GW), GW)

        def times(k, target):
            return weight[k, pl.ds(g * GRP + target + GRP, 1), :]

        def part(block, source, target=0):
            return block[source * R : (source + 1) * R, target * PT : (target + 1) * PT]

        x = xd[pl.ds(pl.multiple_of(g * 128, 128), 128), :]
        x_next = xd[pl.ds(pl.multiple_of(g * 128 + 128, 128), 128), :]
        own = [part(oe[:, here], 0, j) for j in range(GRP)]
        nugget = xe[:, there].astype(F32)
        following = [part(nugget, 0, j) for j in range(GRP)]
        for j in range(GRP):
            n = j + 1
            to_later = dot(x[: n * R, : n * PT], inner[: n * PT, j * PT : (j + 1) * PT])
            for i in range(n):
                own[j] = own[j] + times(GRP + i, j) * part(to_later, i)
        for i in range(GRP - 1):
            n = i + 1
            to_earlier = dot_nt(x[n * R :, n * PT :], inner[i * PT : n * PT, n * PT :])
            for j in range(n, GRP):
                own[i] = own[i] + times(GRP + j, i) * part(to_earlier, j - n)
        forth, back = dot(x, cross[...]), dot_nt(x_next, cross[...])
        for j in range(GRP):
            for i in range(GRP):
                following[j] = following[j] + times(i, GRP + j) * part(forth, i, j)
                own[i] = own[i] + times(2 * GRP + j, i) * part(back, j, i)
        oe[:, here] = jnp.concatenate(own, axis=1)
        oe[:, there] = jnp.concatenate(following, axis=1)

    for copy in coup_copies:
        copy.wait()
    middle_row = lax.broadcasted_iota(jnp.int32, (1, 8, 128), 1)
    middle = jnp.where(
        middle_row == 2,
        (me * GROUPS + GROUPS // 2).astype(F32),
        jnp.where(middle_row < 2, 1.0, 0.0),
    )

    def put_leaves(where, cen, rad):
        u, v = features(SCALE * (cen - middle + rad * units[None]), 1)
        v_all[pl.ds(where, 8)] = v.astype(BF16)
        return u

    def put_coefs(where, two):
        other = pltpu.roll(two, K, 1)
        c_all[where] = jnp.where(lane_half, two, other).astype(BF16)
        c_all[where + 1] = jnp.where(lane_half, other, two).astype(BF16)

    def coupling_side(b):
        u = put_leaves(REACH + b * 8, centers[pl.ds(b * 8, 8)], radii[pl.ds(b * 8, 8)])
        up_pair[pl.ds(b * 4, 4)] = side_by_side(u).astype(BF16)
        for s in range(4):
            put_coefs(REACH + b * 8 + 2 * s, pairs[b * 4 + s])
        side, eighth = b // 8, lax.rem(b, 8)
        start = side * (REACH + LD) + eighth * 8
        turn = lax.rem(LD + side * REACH + REACH - eighth * 8, LD)
        shape = pltpu.roll(halo_shape[side], turn, 1)
        cens = [jnp.broadcast_to(shape[0:8, s : s + 1], (8, 128)) for s in range(8)]
        rads = [jnp.broadcast_to(shape[8:16, s : s + 1], (8, 128)) for s in range(8)]
        put_leaves(start, jnp.stack(cens), jnp.stack(rads))
        for s in range(4):
            put_coefs(start + 2 * s, halo_coef[side, eighth * 4 + s].astype(F32))

    def siblings(b):
        for s in range(4):
            i = jnp.minimum(b * 4 + s, LD // 2 - 2)
            sib[i] = couple_near_pair(pairs[LD // 2 + i], pair_co[i])

    for g in range(4):
        near_features(g)
    near_tiles(0, inner0, cross0)

    @pl.loop(0, GROUPS // 2)
    def _(h):
        near_tiles(2 * h + 1, inner1, cross1)
        near_sums(2 * h, inner0, cross0)
        near_tiles(2 * h + 2, inner0, cross0)
        near_sums(2 * h + 1, inner1, cross1)
        for s in range(2):
            near_features(jnp.minimum(2 * h + 4 + s, GROUPS + 1))
        coupling_side(h)
        siblings(h)

    near_sums(GROUPS, inner0, cross0)

    def climb(got, width, level0, index):
        coefs = got[:, 0:R, :]
        cen, rad = unpacked_shape(got[:, R : R + 8, :])
        level = level0
        while width > 1:
            two = side_by_side(coefs)
            path_pair[level, pl.ds(0, width // 2)] = two
            path_co[level, pl.ds(0, width // 2)] = pair_coords(cen, rad, units)
            coefs = lift(two)
            cen, rad = merge_shapes(cen, rad)
            width //= 2
            level += 1
        return coefs[0], packed_shape(cen[0], rad[0])

    sub_levels, leaf_levels = ns.bit_length() - 1, nl.bit_length() - 1
    for copy in sub_copies:
        copy.wait()
    top_coef, top_shape = climb(got_sub[...], ns, 0, sub_id)
    root_b[0:R, :] = top_coef
    root_b[R : R + 8, :] = top_shape
    leaf_copies = [
        send(root_b, got_leaf.at[leaf_id], leaf_send.at[o], leaf_recv.at[o], device)
        for o, device in enumerate(leaf_devs)
    ]
    got_leaf[leaf_id] = root_b[...]

    dead = LD + 2 * REACH
    for ref in (c_all, v_all):
        ref[dead] = jnp.zeros(ref.shape[1:], BF16)
    first_half = lower_lanes((FEAT, 128))

    def listed(m):
        u = jnp.transpose(up_pair[m].astype(F32)).astype(BF16)
        tiles, sources = [], []
        for s in range(2):
            leaf = 2 * m + s
            vs, cs = [], []
            for t in range(4):
                picked = []
                for slot in (2 * t, 2 * t + 1):
                    j = coupling_list[slot, leaf]
                    near_by = jnp.clip(j - first + REACH, 0, dead - 1)
                    picked.append(jnp.where(j >= 0, near_by, dead))
                vs.append(jnp.where(first_half, v_all[picked[0]], v_all[picked[1]]))
                cs.append(jnp.where(first_half, c_all[picked[0]], c_all[picked[1]]))
            d2 = dot(u[s * K : (s + 1) * K], jnp.concatenate(vs, axis=1))
            tiles.append(from_square(d2).astype(BF16))
            sources.append(jnp.concatenate(cs, axis=1))
        return jnp.concatenate(sources, axis=0), jnp.concatenate(tiles, axis=0)

    @pl.loop(0, LD // 8)
    def _(b):
        operands = [listed(b * 4 + s) for s in range(4)]
        for s in range(4):
            product = dot_nt(*operands[s])
            lc[b * 4 + s] = jnp.where(lane_half, product[:R], product[R:])

    for copy in leaf_copies:
        copy.wait()
    climb(got_leaf[...], nl, sub_levels, leaf_id)

    def masked(pair, side):
        chosen = lower_lanes(pair.shape) == (side == 0)
        return jnp.where(chosen, pair, 0.0)

    held = None
    for level in reversed(range(sub_levels + leaf_levels)):
        position = (sub_id if level < sub_levels else leaf_id)
        shift = level if level < sub_levels else level - sub_levels
        node = position // (2**shift)
        pair = node // 2
        mine = couple_pair(path_pair[level, pair], path_co[level, pair])
        if held is not None:
            mine = mine + dot3(held, down_high, down_low)
        held = masked(mine, lax.rem(node, 2))

    def spread(pair_block):
        n = pair_block.shape[0]
        lower = lower_lanes(pair_block.shape)
        both = jnp.stack(
            [jnp.where(lower, pair_block, 0.0), jnp.where(lower, 0.0, pair_block)], axis=1
        )
        return dot3(both.reshape(2 * n * R, 128), down_high, down_low).reshape(2 * n, R, 128)

    n, offset = 1, LD // 2 - 2
    block = sib[pl.ds(offset, 1)] + dot3(held, down_high, down_low)[None]
    while n < LD // 4:
        block = spread(block)
        n *= 2
        offset -= n
        block = block + sib[pl.ds(offset, n)]
    d1[...] = block

    @pl.loop(0, LD // 16)
    def _(b):
        below = spread(d1[pl.ds(b * 4, 4)])
        for s in range(8):
            m = b * 8 + s
            coef = lc[m] + below[s]
            stacked = jnp.concatenate(
                [jnp.where(lane_half, coef, 0.0), jnp.where(lane_half, 0.0, coef)], axis=0
            ).astype(BF16)
            far = dot(stacked, basis[pl.ds(2 * m, 2)].reshape(2 * K, PT))
            start = pl.multiple_of(m * 256, 256)
            near = oe[:, pl.ds(pl.multiple_of(GW + m * 256, 256), 256)]
            out[:, pl.ds(start, 256)] = near + jnp.concatenate([far[:R], far[R:]], axis=1)


def per_device(charges, points, basis, transfer, near_list, coupling_list):
    nl, ns = lax.axis_size("leaf"), lax.axis_size("sub")
    levels = (nl * ns).bit_length() - 1
    widest = max(nl, ns) // 2
    vmem = pl.BlockSpec(memory_space=pltpu.VMEM)
    total = LD + 2 * REACH + 1

    def body(*refs):
        kernel(nl, ns, *refs)

    dma = pltpu.SemaphoreType.DMA
    return pl.pallas_call(
        body,
        out_shape=jax.ShapeDtypeStruct((R, LD * PT), F32),
        in_specs=[vmem] * 5 + [pl.BlockSpec(memory_space=pltpu.SMEM)],
        out_specs=vmem,
        scratch_shapes=[
            pltpu.VMEM((8, EXT), F32),
            pltpu.VMEM((R, EXT), BF16),
            pltpu.VMEM((R, EXT), F32),
            pltpu.VMEM((FEAT, EXT), BF16),
            pltpu.VMEM((FEAT, EXT), BF16),
            pltpu.VMEM((FEAT, EXT), BF16),
            pltpu.VMEM(((GROUPS + 2) * 128, GW), BF16),
            pltpu.VMEM((GW, GW), BF16),
            pltpu.VMEM((GW, GW), BF16),
            pltpu.VMEM((GW, GW), BF16),
            pltpu.VMEM((GW, GW), BF16),
            pltpu.VMEM((3 * GRP, LD + 16, 128), F32),
            pltpu.VMEM((LD, 8, 128), F32),
            pltpu.VMEM((LD, 8, 128), F32),
            pltpu.VMEM((LD, R, 128), F32),
            pltpu.VMEM((LD // 2, 8, 128), F32),
            pltpu.VMEM((LD // 2, R, 128), F32),
            pltpu.VMEM((LD // 2, FEAT, 128), BF16),
            pltpu.VMEM((total, FEAT, 128), BF16),
            pltpu.VMEM((total, R, 128), BF16),
            pltpu.VMEM((LD // 2, R, 128), F32),
            pltpu.VMEM((LD // 2, R, 128), BF16),
            pltpu.VMEM((2, REACH // 2, R, 128), BF16),
            pltpu.VMEM((16, 128), F32),
            pltpu.VMEM((2, 16, 128), F32),
            pltpu.VMEM((R + 8, 128), F32),
            pltpu.VMEM((ns, R + 8, 128), F32),
            pltpu.VMEM((R + 8, 128), F32),
            pltpu.VMEM((nl, R + 8, 128), F32),
            pltpu.VMEM((levels, widest, R, 128), F32),
            pltpu.VMEM((levels, widest, 8, 128), F32),
            pltpu.VMEM((LD // 4, R, 128), F32),
            dma((4,)), dma((4,)), dma((4,)), dma((4,)),
            dma((ns,)), dma((ns,)), dma((nl,)), dma((nl,)), dma((1,)),
        ],
        compiler_params=pltpu.CompilerParams(
            collective_id=0, has_side_effects=True, vmem_limit_bytes=56 * 2**20
        ),
        cost_estimate=pl.CostEstimate(
            flops=6 * 10**9, bytes_accessed=7 * 10**6, transcendentals=4 * 10**7
        ),
    )(charges, points, basis, transfer, near_list.T, coupling_list.T)


def solution(mesh):
    in_specs = (
        P(None, ("leaf", "sub")),
        P(None, ("leaf", "sub")),
        P(("leaf", "sub"), None, None),
        P(),
        P(("leaf", "sub"), None),
        P(("leaf", "sub"), None),
    )
    return jax.shard_map(
        per_device,
        mesh=mesh,
        in_specs=in_specs,
        out_specs=P(None, ("leaf", "sub")),
        check_vma=False,
    )
```

```python
import math

import jax
import jax.numpy as jnp
from jax import lax
from jax.experimental import pallas as pl
from jax.experimental.pallas import tpu as pltpu
from jax.sharding import PartitionSpec as P

F32, BF16 = jnp.float32, jnp.bfloat16
PT = 128
K = 64
R = 32
LD = 128
REACH = 64
GRP = 4
GW = GRP * PT
GROUPS = LD // GRP
EXT = (GROUPS + 2) * GW
FEAT = 32
SCALE = math.log2(math.e) / 2.0
TINY = 1e-30
MESH = pl.DeviceIdType.MESH


def dot(a, b):
    return lax.dot_general(a, b, (((1,), (0,)), ((), ())), preferred_element_type=F32)


def dot_nt(a, b):
    return lax.dot_general(a, b, (((1,), (1,)), ((), ())), preferred_element_type=F32)


def dot_tn(a, b):
    return lax.dot_general(a, b, (((0,), (0,)), ((), ())), preferred_element_type=F32)


def split2(x):
    high = x.astype(BF16)
    return high, (x - high.astype(F32)).astype(BF16)


def dot3(a, b_high, b_low):
    high, low = split2(a)
    n = a.shape[0]
    both = dot(jnp.concatenate([high, low], axis=0), b_high)
    return both[:n] + (dot(high, b_low) + both[n:])


def from_square(d2):
    x = jnp.maximum(d2, TINY)
    return jnp.exp2(-(x * lax.rsqrt(x)))


def features(coords, axis):
    high = coords.astype(BF16).astype(F32)
    low = (coords - high).astype(BF16).astype(F32)
    kept = high + low
    norm = jnp.sum(kept * kept, axis=axis, keepdims=True)
    n1 = norm.astype(BF16).astype(F32)
    n2 = (norm - n1).astype(BF16).astype(F32)
    n3 = norm - n1 - n2
    row = lax.broadcasted_iota(jnp.int32, coords.shape, axis)
    ones = jnp.where((row >= 4) & (row < 7), 1.0, 0.0)
    norms = jnp.where(row == 0, n1, jnp.where(row == 1, n2, jnp.where(row == 2, n3, ones)))
    both = high + pltpu.roll(low, 4, axis)
    twice = -2.0 * both
    zero = jnp.zeros_like(both)
    u = jnp.concatenate([both, both, norms, zero], axis=axis)
    v = jnp.concatenate(
        [twice, pltpu.roll(twice, 4, axis), pltpu.roll(norms, 4, axis), zero], axis=axis
    )
    return u, v


def unit_rows():
    row = lax.broadcasted_iota(jnp.int32, (8, 128), 0)
    index = lax.broadcasted_iota(jnp.int32, (8, 128), 1) % K
    digit = jnp.where(row == 0, index // 16, jnp.where(row == 1, index // 4 % 4, index % 4))
    big, small = math.cos(math.pi / 8.0), math.cos(3.0 * math.pi / 8.0)
    value = jnp.where(
        digit == 0, big, jnp.where(digit == 1, small, jnp.where(digit == 2, -small, -big))
    )
    return jnp.where(row < 3, value, 0.0).astype(F32)


def lower_lanes(shape):
    return lax.broadcasted_iota(jnp.int32, shape, len(shape) - 1) < K


def halves(x):
    paired = x.reshape((x.shape[0] // 2, 2) + x.shape[1:])
    return paired[:, 0], paired[:, 1]


def side_by_side(x):
    left, right = halves(x)
    return jnp.where(lower_lanes(left.shape), left, right)


def merge_shapes(centers, radii):
    c0, c1 = halves(centers)
    r0, r1 = halves(radii)
    gap = c0 - c1
    reach = jnp.sqrt(jnp.sum(gap * gap, axis=1, keepdims=True))
    return 0.5 * (c0 + c1), jnp.maximum(r0, r1) + 0.5 * reach


def pair_coords(centers, radii, units):
    c0, c1 = halves(centers)
    r0, r1 = halves(radii)
    half = 0.5 * (c0 - c1)
    left = lower_lanes(half.shape)
    return SCALE * (jnp.where(left, half, -half) + jnp.where(left, r0, r1) * units[None])


def couple_pair(coefs, coords):
    u, v = features(coords, 0)
    lower = lower_lanes(v.shape)
    v_two = jnp.concatenate([jnp.where(lower, v, 0.0), jnp.where(lower, 0.0, v)], axis=0)
    columns = jnp.transpose(u)
    u_two = jnp.concatenate([columns[K:], columns[:K]], axis=1)
    tile_high, tile_low = split2(from_square(dot(u_two.astype(BF16), v_two.astype(BF16))))
    swapped = pltpu.roll(coefs, K, 1)
    both = dot3(jnp.concatenate([swapped[:, :K], coefs[:, :K]], axis=0), tile_high, tile_low)
    return jnp.where(lower_lanes((R, 128)), both[:R], both[R:])


def block_diagonal(x):
    leaf = lax.broadcasted_iota(jnp.int32, x.shape, 1) // PT
    wide = x.astype(F32)
    return jnp.concatenate(
        [jnp.where(leaf == k, wide, 0.0) for k in range(GRP)], axis=0
    ).astype(BF16)


def kernel(
    nl, ns,
    charges, points, basis_hbm, transfer, near_list, coupling_list,
    out_hbm,
    basis, out, p8, xe, oe, ua, va, vb, xd, inner0, cross0, inner1, cross1, weight,
    centers, radii, pairs, pair_co, sib,
    up_pair, v_all, c_all, lc,
    send_coef, halo_coef, send_shape, halo_shape,
    root, got_sub, root_b, got_leaf, path_pair, path_co, d1,
    near_send, near_recv, coup_send, coup_recv, sub_send, sub_recv, leaf_send, leaf_recv, local_sem, out_sem,
):
    leaf_id, sub_id = lax.axis_index("leaf"), lax.axis_index("sub")
    count = nl * ns
    me = leaf_id * ns + sub_id
    right, left = lax.rem(me + 1, count), lax.rem(me + count - 1, count)
    left_dev = (left // ns, lax.rem(left, ns))
    right_dev = (right // ns, lax.rem(right, ns))
    sub_devs = [(leaf_id, lax.rem(sub_id + o, ns)) for o in range(1, ns)]
    leaf_devs = [(lax.rem(leaf_id + o, nl), sub_id) for o in range(1, nl)]
    barrier = pltpu.get_barrier_semaphore()
    partners = [left_dev, right_dev] + sub_devs + leaf_devs
    for device in partners:
        pl.semaphore_signal(barrier, inc=1, device_id=device, device_id_type=MESH)

    def send(src, dst, send_sem, recv_sem, device):
        copy = pltpu.make_async_remote_copy(
            src_ref=src, dst_ref=dst, send_sem=send_sem, recv_sem=recv_sem,
            device_id=device, device_id_type=MESH,
        )
        copy.start()
        return copy

    own_charges = pltpu.make_async_copy(
        charges, xe.at[:, pl.ds(GW, LD * PT)], local_sem.at[0]
    )
    own_charges.start()
    own_basis = pltpu.make_async_copy(basis_hbm, basis, local_sem.at[1])
    own_basis.start()
    first = me * LD
    units = unit_rows()
    lane_half = lower_lanes((R, 128))

    p8[3:8, GW : EXT - GW] = jnp.zeros((5, LD * PT), F32)
    p8[0:3, GW : EXT - GW] = points[...]

    own_charges.wait()
    pl.semaphore_wait(barrier, len(partners))
    copies = []
    copies.append(send(xe.at[:, pl.ds(GW, GW)], xe.at[:, pl.ds(EXT - GW, GW)],
                       near_send.at[0], near_recv.at[0], left_dev))
    copies.append(send(xe.at[:, pl.ds(EXT - 2 * GW, GW)], xe.at[:, pl.ds(0, GW)],
                       near_send.at[1], near_recv.at[1], right_dev))
    copies.append(send(p8.at[:, pl.ds(GW, GW)], p8.at[:, pl.ds(EXT - GW, GW)],
                       near_send.at[2], near_recv.at[2], left_dev))
    copies.append(send(p8.at[:, pl.ds(EXT - 2 * GW, GW)], p8.at[:, pl.ds(0, GW)],
                       near_send.at[3], near_recv.at[3], right_dev))
    near_copies = copies

    @pl.loop(0, LD // 32)
    def _(block):
        start = pl.multiple_of(GW + block * (32 * PT), GW)
        wide = p8[:, pl.ds(start, 32 * PT)]
        pts = jnp.stack([wide[:, c * PT : (c + 1) * PT] for c in range(32)])
        rows = pl.ds(block * 32, 32)
        center = jnp.mean(pts, axis=2, keepdims=True)
        off = pts - center
        far = jnp.max(jnp.sum(off * off, axis=1, keepdims=True), axis=2, keepdims=True)
        centers[rows] = jnp.broadcast_to(center, pts.shape)
        radii[rows] = jnp.broadcast_to(jnp.sqrt(far), pts.shape)

    row8 = lax.broadcasted_iota(jnp.int32, (8, 128), 0)
    lane8 = lax.broadcasted_iota(jnp.int32, (8, 128), 1)

    packed_cen, packed_rad = centers[0], radii[0]
    for c in range(1, LD):
        packed_cen = jnp.where(lane8 == c, centers[c], packed_cen)
        packed_rad = jnp.where(lane8 == c, radii[c], packed_rad)
    send_shape[0:8, :] = packed_cen
    send_shape[8:16, :] = packed_rad

    own_basis.wait()

    @pl.loop(0, LD // 32)
    def _(block):
        for s in range(16):
            m = block * 16 + s
            x = xe[:, pl.ds(pl.multiple_of(GW + m * 256, 256), 256)]
            stacked = jnp.concatenate([x[:, :128], x[:, 128:]], axis=0)
            both = basis[pl.ds(2 * m, 2)].reshape(2 * K, PT)
            product = dot_nt(stacked, both)
            pair = jnp.where(lane_half, product[:R], product[R:])
            pairs[m] = pair
            send_coef[m] = pair.astype(BF16)

    half_pairs = REACH // 2
    coup_copies = [
        send(send_coef.at[pl.ds(0, half_pairs)], halo_coef.at[1],
             coup_send.at[0], coup_recv.at[0], left_dev),
        send(send_coef.at[pl.ds(half_pairs, half_pairs)], halo_coef.at[0],
             coup_send.at[1], coup_recv.at[1], right_dev),
        send(send_shape, halo_shape.at[1], coup_send.at[2], coup_recv.at[2], left_dev),
        send(send_shape, halo_shape.at[0], coup_send.at[3], coup_recv.at[3], right_dev),
    ]

    t0, t1 = transfer[0], transfer[1]
    up = jnp.concatenate([t0, t1], axis=0)
    up_high, up_low = split2(jnp.concatenate([up, up], axis=1))
    down = jnp.concatenate([jnp.transpose(t0), jnp.transpose(t1)], axis=1)
    down_high, down_low = split2(jnp.concatenate([down, down], axis=0))

    def lift(pair_block):
        n = pair_block.shape[0]
        return dot3(pair_block.reshape(n * R, 128), up_high, up_low).reshape(n, R, 128)

    level_cen, level_rad = centers[...], radii[...]
    offset, n = 0, LD // 2
    block = None
    while n > 1:
        level_cen, level_rad = merge_shapes(level_cen, level_rad)
        if n >= 32:

            def lift_part(i, offset=offset, n=n):
                eight = pairs[pl.ds(offset + i * 8, 8)]
                pairs[pl.ds(offset + n + i * 4, 4)] = side_by_side(lift(eight))

            pl.loop(0, n // 8)(lift_part)
        else:
            if block is None:
                block = pairs[pl.ds(offset, n)]
            block = side_by_side(lift(block))
            pairs[pl.ds(offset + n, n // 2)] = block
        offset += n
        n //= 2
        pair_co[pl.ds(offset - LD // 2, n)] = pair_coords(level_cen, level_rad, units)
    root_coef = lift(block)[0]
    root_cen, root_rad = merge_shapes(level_cen, level_rad)

    def packed_shape(cen, rad):
        return jnp.where(row8 < 3, cen, rad)

    def unpacked_shape(shape):
        rows = lax.broadcasted_iota(jnp.int32, shape.shape, 1)
        cen = jnp.where(rows < 3, shape, 0.0)
        rad = jnp.sum(jnp.where(rows == 3, shape, 0.0), axis=1, keepdims=True)
        return cen, jnp.broadcast_to(rad, shape.shape)

    root[0:R, :] = root_coef
    root[R : R + 8, :] = packed_shape(root_cen[0], root_rad[0])
    sub_copies = [
        send(root, got_sub.at[sub_id], sub_send.at[o], sub_recv.at[o], device)
        for o, device in enumerate(sub_devs)
    ]
    got_sub[sub_id] = root[...]

    leaf_lane = lax.broadcasted_iota(jnp.int32, (8, LD), 1)
    base = first + (leaf_lane // GRP) * GRP - GRP
    listed_leaf = near_list[...]
    relative = jnp.where(listed_leaf >= 0, listed_leaf - base, -1)
    slot_row = lax.broadcasted_iota(jnp.int32, (16, LD), 0)
    counts = jnp.zeros((16, LD), F32)
    for k in range(3 * GRP):
        times = jnp.sum(jnp.where(relative == k, 1.0, 0.0), axis=0, keepdims=True)
        counts = jnp.where(slot_row == k, times, counts)
    columns = jnp.transpose(counts).astype(BF16)
    for k in range(3 * GRP):
        ones = jnp.where(slot_row == k, 1.0, 0.0).astype(BF16)
        weight[k, 0:8, :] = jnp.zeros((8, 128), F32)
        weight[k, 8 : 8 + LD, :] = dot(columns, ones)
        weight[k, 8 + LD : 16 + LD, :] = jnp.zeros((8, 128), F32)

    for copy in near_copies:
        copy.wait()

    def near_features(g):
        lanes = pl.ds(pl.multiple_of(g * GW, GW), GW)
        row = lax.broadcasted_iota(jnp.int32, (8, GW), 0)
        z0 = lax.convert_element_type(me * GROUPS + g - 1, F32)
        corner = jnp.where(row == 2, z0, jnp.where(row < 2, 1.0, 0.0))
        low = p8[:, lanes] - corner
        shift = jnp.where(row == 2, 1.0, 0.0)
        u, v = features(SCALE * (low - shift), 0)
        ua[:, lanes] = u.astype(BF16)
        va[:, lanes] = v.astype(BF16)
        vb[:, lanes] = features(SCALE * low, 0)[1].astype(BF16)
        xd[pl.ds(pl.multiple_of(g * 128, 128), 128), :] = block_diagonal(xe[:, lanes])

    oe[:, 0:GW] = jnp.zeros((R, GW), F32)

    def near_tiles(g, inner, cross):
        here = pl.ds(pl.multiple_of(g * GW, GW), GW)
        there = pl.ds(pl.multiple_of(g * GW + GW, GW), GW)
        u, v, v_next = ua[:, here], va[:, here], vb[:, there]
        for i in range(GRP):
            rows = slice(i * PT, (i + 1) * PT)
            inner[rows, i * PT :] = from_square(dot_tn(u[:, rows], v[:, i * PT :])).astype(BF16)
            cross[rows, :] = from_square(dot_tn(u[:, rows], v_next)).astype(BF16)

    def near_sums(g, inner, cross):
        here = pl.ds(pl.multiple_of(g * GW, GW), GW)
        there = pl.ds(pl.multiple_of(g * GW + GW, GW), GW)

        def times(k, target):
            return weight[k, pl.ds(g * GRP + target + GRP, 1), :]

        def part(block, source, target=0):
            return block[source * R : (source + 1) * R, target * PT : (target + 1) * PT]

        x = xd[pl.ds(pl.multiple_of(g * 128, 128), 128), :]
        x_next = xd[pl.ds(pl.multiple_of(g * 128 + 128, 128), 128), :]
        own = [part(oe[:, here], 0, j) for j in range(GRP)]
        nugget = xe[:, there].astype(F32)
        following = [part(nugget, 0, j) for j in range(GRP)]
        for j in range(GRP):
            n = j + 1
            to_later = dot(x[: n * R, : n * PT], inner[: n * PT, j * PT : (j + 1) * PT])
            for i in range(n):
                own[j] = own[j] + times(GRP + i, j) * part(to_later, i)
        for i in range(GRP - 1):
            n = i + 1
            to_earlier = dot_nt(x[n * R :, n * PT :], inner[i * PT : n * PT, n * PT :])
            for j in range(n, GRP):
                own[i] = own[i] + times(GRP + j, i) * part(to_earlier, j - n)
        forth, back = dot(x, cross[...]), dot_nt(x_next, cross[...])
        for j in range(GRP):
            for i in range(GRP):
                following[j] = following[j] + times(i, GRP + j) * part(forth, i, j)
                own[i] = own[i] + times(2 * GRP + j, i) * part(back, j, i)
        oe[:, here] = jnp.concatenate(own, axis=1)
        oe[:, there] = jnp.concatenate(following, axis=1)

    middle_row = lax.broadcasted_iota(jnp.int32, (1, 8, 128), 1)
    middle = jnp.where(
        middle_row == 2,
        (me * GROUPS + GROUPS // 2).astype(F32),
        jnp.where(middle_row < 2, 1.0, 0.0),
    )

    def put_leaves(where, cen, rad):
        u, v = features(SCALE * (cen - middle + rad * units[None]), 1)
        v_all[pl.ds(where, 8)] = v.astype(BF16)
        return u

    def put_coefs(where, two):
        other = pltpu.roll(two, K, 1)
        c_all[where] = jnp.where(lane_half, two, other).astype(BF16)
        c_all[where + 1] = jnp.where(lane_half, other, two).astype(BF16)

    def coupling_own(b):
        u = put_leaves(REACH + b * 8, centers[pl.ds(b * 8, 8)], radii[pl.ds(b * 8, 8)])
        up_pair[pl.ds(b * 4, 4)] = side_by_side(u).astype(BF16)
        for s in range(4):
            put_coefs(REACH + b * 8 + 2 * s, pairs[b * 4 + s])

    def coupling_halo(side, b):
        start = side * (REACH + LD) + b * 8
        turn = lax.rem(LD + (1 - side) * REACH - b * 8, LD)
        shape = pltpu.roll(halo_shape[side], turn, 1)
        cens = [jnp.broadcast_to(shape[0:8, s : s + 1], (8, 128)) for s in range(8)]
        rads = [jnp.broadcast_to(shape[8:16, s : s + 1], (8, 128)) for s in range(8)]
        put_leaves(start, jnp.stack(cens), jnp.stack(rads))
        for s in range(4):
            put_coefs(start + 2 * s, halo_coef[side, b * 4 + s].astype(F32))

    def siblings(b):
        for s in range(4):
            i = jnp.minimum(b * 4 + s, LD // 2 - 2)
            sib[i] = couple_pair(pairs[LD // 2 + i], pair_co[i])

    for g in range(4):
        near_features(g)
    near_tiles(0, inner0, cross0)

    def near_turn(h):
        near_tiles(2 * h + 1, inner1, cross1)
        near_sums(2 * h, inner0, cross0)
        near_tiles(2 * h + 2, inner0, cross0)
        near_sums(2 * h + 1, inner1, cross1)
        for s in range(2):
            near_features(jnp.minimum(2 * h + 4 + s, GROUPS + 1))
        siblings(h)

    @pl.loop(0, GROUPS // 4)
    def _(h):
        near_turn(h)
        coupling_own(2 * h)
        coupling_own(2 * h + 1)

    for copy in coup_copies:
        copy.wait()

    @pl.loop(0, GROUPS // 4)
    def _(h):
        near_turn(GROUPS // 4 + h)
        coupling_halo(0, h)
        coupling_halo(1, h)

    near_sums(GROUPS, inner0, cross0)

    def climb(got, width, level0, index):
        coefs = got[:, 0:R, :]
        cen, rad = unpacked_shape(got[:, R : R + 8, :])
        level = level0
        while width > 1:
            two = side_by_side(coefs)
            path_pair[level, pl.ds(0, width // 2)] = two
            path_co[level, pl.ds(0, width // 2)] = pair_coords(cen, rad, units)
            coefs = lift(two)
            cen, rad = merge_shapes(cen, rad)
            width //= 2
            level += 1
        return coefs[0], packed_shape(cen[0], rad[0])

    sub_levels, leaf_levels = ns.bit_length() - 1, nl.bit_length() - 1
    for copy in sub_copies:
        copy.wait()
    top_coef, top_shape = climb(got_sub[...], ns, 0, sub_id)
    root_b[0:R, :] = top_coef
    root_b[R : R + 8, :] = top_shape
    leaf_copies = [
        send(root_b, got_leaf.at[leaf_id], leaf_send.at[o], leaf_recv.at[o], device)
        for o, device in enumerate(leaf_devs)
    ]
    got_leaf[leaf_id] = root_b[...]

    dead = LD + 2 * REACH
    for ref in (c_all, v_all):
        ref[dead] = jnp.zeros(ref.shape[1:], BF16)
    first_half = lower_lanes((FEAT, 128))

    def listed(m):
        u = jnp.transpose(up_pair[m].astype(F32)).astype(BF16)
        tiles, sources = [], []
        for s in range(2):
            leaf = 2 * m + s
            vs, cs = [], []
            for t in range(4):
                picked = []
                for slot in (2 * t, 2 * t + 1):
                    j = coupling_list[slot, leaf]
                    near_by = jnp.clip(j - first + REACH, 0, dead - 1)
                    picked.append(jnp.where(j >= 0, near_by, dead))
                vs.append(jnp.where(first_half, v_all[picked[0]], v_all[picked[1]]))
                cs.append(jnp.where(first_half, c_all[picked[0]], c_all[picked[1]]))
            d2 = dot(u[s * K : (s + 1) * K], jnp.concatenate(vs, axis=1))
            tiles.append(from_square(d2).astype(BF16))
            sources.append(jnp.concatenate(cs, axis=1))
        return jnp.concatenate(sources, axis=0), jnp.concatenate(tiles, axis=0)

    def couple_four(b):
        operands = [listed(b * 4 + s) for s in range(4)]
        for s in range(4):
            product = dot_nt(*operands[s])
            lc[b * 4 + s] = jnp.where(lane_half, product[:R], product[R:])

    beside = 2
    pl.loop(0, LD // 8 - beside)(couple_four)

    for copy in leaf_copies:
        copy.wait()
    climb(got_leaf[...], nl, sub_levels, leaf_id)

    def masked(pair, side):
        chosen = lower_lanes(pair.shape) == (side == 0)
        return jnp.where(chosen, pair, 0.0)

    held = None
    for level in reversed(range(sub_levels + leaf_levels)):
        position = (sub_id if level < sub_levels else leaf_id)
        shift = level if level < sub_levels else level - sub_levels
        node = position // (2**shift)
        pair = node // 2
        mine = couple_pair(path_pair[level, pair], path_co[level, pair])
        if held is not None:
            mine = mine + dot3(held, down_high, down_low)
        held = masked(mine, lax.rem(node, 2))

    def spread(pair_block):
        n = pair_block.shape[0]
        lower = lower_lanes(pair_block.shape)
        both = jnp.stack(
            [jnp.where(lower, pair_block, 0.0), jnp.where(lower, 0.0, pair_block)], axis=1
        )
        return dot3(both.reshape(2 * n * R, 128), down_high, down_low).reshape(2 * n, R, 128)

    n, offset = 1, LD // 2 - 2
    block = sib[pl.ds(offset, 1)] + dot3(held, down_high, down_low)[None]
    while n < LD // 4:
        block = spread(block)
        n *= 2
        offset -= n
        block = block + sib[pl.ds(offset, n)]
    d1[...] = block
    for b in range(LD // 8 - beside, LD // 8):
        couple_four(b)

    def put_out(b):
        lanes = pl.ds(pl.multiple_of(b * 32 * PT, 32 * PT), 32 * PT)
        return pltpu.make_async_copy(out.at[:, lanes], out_hbm.at[:, lanes], out_sem.at[b])

    @pl.loop(0, LD // 32)
    def _(b):
        below = spread(d1[pl.ds(b * 8, 8)])
        for s in range(16):
            m = b * 16 + s
            coef = lc[m] + below[s]
            stacked = jnp.concatenate(
                [jnp.where(lane_half, coef, 0.0), jnp.where(lane_half, 0.0, coef)], axis=0
            ).astype(BF16)
            far = dot(stacked, basis[pl.ds(2 * m, 2)].reshape(2 * K, PT))
            start = pl.multiple_of(m * 256, 256)
            near = oe[:, pl.ds(pl.multiple_of(GW + m * 256, 256), 256)]
            out[:, pl.ds(start, 256)] = near + jnp.concatenate([far[:R], far[R:]], axis=1)
        put_out(b).start()

    for b in range(LD // 32):
        put_out(b).wait()


def per_device(charges, points, basis, transfer, near_list, coupling_list):
    nl, ns = lax.axis_size("leaf"), lax.axis_size("sub")
    levels = (nl * ns).bit_length() - 1
    widest = max(nl, ns) // 2
    vmem = pl.BlockSpec(memory_space=pltpu.VMEM)
    hbm = pl.BlockSpec(memory_space=pl.ANY)
    total = LD + 2 * REACH + 1

    def body(*refs):
        kernel(nl, ns, *refs)

    dma = pltpu.SemaphoreType.DMA
    return pl.pallas_call(
        body,
        out_shape=jax.ShapeDtypeStruct((R, LD * PT), F32),
        in_specs=[hbm, vmem, hbm, vmem, vmem, pl.BlockSpec(memory_space=pltpu.SMEM)],
        out_specs=hbm,
        scratch_shapes=[
            pltpu.VMEM((LD, K, PT), BF16),
            pltpu.VMEM((R, LD * PT), F32),
            pltpu.VMEM((8, EXT), F32),
            pltpu.VMEM((R, EXT), BF16),
            pltpu.VMEM((R, EXT), F32),
            pltpu.VMEM((FEAT, EXT), BF16),
            pltpu.VMEM((FEAT, EXT), BF16),
            pltpu.VMEM((FEAT, EXT), BF16),
            pltpu.VMEM(((GROUPS + 2) * 128, GW), BF16),
            pltpu.VMEM((GW, GW), BF16),
            pltpu.VMEM((GW, GW), BF16),
            pltpu.VMEM((GW, GW), BF16),
            pltpu.VMEM((GW, GW), BF16),
            pltpu.VMEM((3 * GRP, LD + 16, 128), F32),
            pltpu.VMEM((LD, 8, 128), F32),
            pltpu.VMEM((LD, 8, 128), F32),
            pltpu.VMEM((LD, R, 128), F32),
            pltpu.VMEM((LD // 2, 8, 128), F32),
            pltpu.VMEM((LD // 2, R, 128), F32),
            pltpu.VMEM((LD // 2, FEAT, 128), BF16),
            pltpu.VMEM((total, FEAT, 128), BF16),
            pltpu.VMEM((total, R, 128), BF16),
            pltpu.VMEM((LD // 2, R, 128), F32),
            pltpu.VMEM((LD // 2, R, 128), BF16),
            pltpu.VMEM((2, REACH // 2, R, 128), BF16),
            pltpu.VMEM((16, 128), F32),
            pltpu.VMEM((2, 16, 128), F32),
            pltpu.VMEM((R + 8, 128), F32),
            pltpu.VMEM((ns, R + 8, 128), F32),
            pltpu.VMEM((R + 8, 128), F32),
            pltpu.VMEM((nl, R + 8, 128), F32),
            pltpu.VMEM((levels, widest, R, 128), F32),
            pltpu.VMEM((levels, widest, 8, 128), F32),
            pltpu.VMEM((LD // 4, R, 128), F32),
            dma((4,)), dma((4,)), dma((4,)), dma((4,)),
            dma((ns,)), dma((ns,)), dma((nl,)), dma((nl,)), dma((2,)), dma((LD // 32,)),
        ],
        compiler_params=pltpu.CompilerParams(
            collective_id=0, has_side_effects=True, vmem_limit_bytes=56 * 2**20
        ),
        cost_estimate=pl.CostEstimate(
            flops=6 * 10**9, bytes_accessed=7 * 10**6, transcendentals=4 * 10**7
        ),
    )(charges, points, basis, transfer, near_list.T, coupling_list.T)


def solution(mesh):
    in_specs = (
        P(None, ("leaf", "sub")),
        P(None, ("leaf", "sub")),
        P(("leaf", "sub"), None, None),
        P(),
        P(("leaf", "sub"), None),
        P(("leaf", "sub"), None),
    )
    return jax.shard_map(
        per_device,
        mesh=mesh,
        in_specs=in_specs,
        out_specs=P(None, ("leaf", "sub")),
        check_vma=False,
    )
```

```python
import math

import jax
import jax.numpy as jnp
from jax import lax
from jax.experimental import pallas as pl
from jax.experimental.pallas import tpu as pltpu
from jax.sharding import PartitionSpec as P

F32, BF16 = jnp.float32, jnp.bfloat16
PT = 128
K = 64
R = 32
LD = 128
REACH = 64
GRP = 4
GW = GRP * PT
GROUPS = LD // GRP
EXT = (GROUPS + 2) * GW
FEAT = 32
SCALE = math.log2(math.e) / 2.0
TINY = 1e-30
MESH = pl.DeviceIdType.MESH


def dot(a, b):
    return lax.dot_general(a, b, (((1,), (0,)), ((), ())), preferred_element_type=F32)


def dot_nt(a, b):
    return lax.dot_general(a, b, (((1,), (1,)), ((), ())), preferred_element_type=F32)


def dot_tn(a, b):
    return lax.dot_general(a, b, (((0,), (0,)), ((), ())), preferred_element_type=F32)


def split2(x):
    high = x.astype(BF16)
    return high, (x - high.astype(F32)).astype(BF16)


def dot3(a, b_high, b_low):
    high, low = split2(a)
    n = a.shape[0]
    both = dot(jnp.concatenate([high, low], axis=0), b_high)
    return both[:n] + (dot(high, b_low) + both[n:])


def from_square(d2):
    x = jnp.maximum(d2, TINY)
    return jnp.exp2(-(x * lax.rsqrt(x)))


def features(coords, axis):
    high = coords.astype(BF16).astype(F32)
    low = (coords - high).astype(BF16).astype(F32)
    kept = high + low
    norm = jnp.sum(kept * kept, axis=axis, keepdims=True)
    n1 = norm.astype(BF16).astype(F32)
    n2 = (norm - n1).astype(BF16).astype(F32)
    n3 = norm - n1 - n2
    row = lax.broadcasted_iota(jnp.int32, coords.shape, axis)
    ones = jnp.where((row >= 4) & (row < 7), 1.0, 0.0)
    norms = jnp.where(row == 0, n1, jnp.where(row == 1, n2, jnp.where(row == 2, n3, ones)))
    both = high + pltpu.roll(low, 4, axis)
    twice = -2.0 * both
    zero = jnp.zeros_like(both)
    u = jnp.concatenate([both, both, norms, zero], axis=axis)
    v = jnp.concatenate(
        [twice, pltpu.roll(twice, 4, axis), pltpu.roll(norms, 4, axis), zero], axis=axis
    )
    return u, v


def unit_rows():
    row = lax.broadcasted_iota(jnp.int32, (8, 128), 0)
    index = lax.broadcasted_iota(jnp.int32, (8, 128), 1) % K
    digit = jnp.where(row == 0, index // 16, jnp.where(row == 1, index // 4 % 4, index % 4))
    big, small = math.cos(math.pi / 8.0), math.cos(3.0 * math.pi / 8.0)
    value = jnp.where(
        digit == 0, big, jnp.where(digit == 1, small, jnp.where(digit == 2, -small, -big))
    )
    return jnp.where(row < 3, value, 0.0).astype(F32)


def lower_lanes(shape):
    return lax.broadcasted_iota(jnp.int32, shape, len(shape) - 1) < K


def halves(x):
    paired = x.reshape((x.shape[0] // 2, 2) + x.shape[1:])
    return paired[:, 0], paired[:, 1]


def side_by_side(x):
    left, right = halves(x)
    return jnp.where(lower_lanes(left.shape), left, right)


def merge_shapes(centers, radii):
    c0, c1 = halves(centers)
    r0, r1 = halves(radii)
    gap = c0 - c1
    reach = jnp.sqrt(jnp.sum(gap * gap, axis=1, keepdims=True))
    return 0.5 * (c0 + c1), jnp.maximum(r0, r1) + 0.5 * reach


def pair_coords(centers, radii, units):
    c0, c1 = halves(centers)
    r0, r1 = halves(radii)
    half = 0.5 * (c0 - c1)
    left = lower_lanes(half.shape)
    return SCALE * (jnp.where(left, half, -half) + jnp.where(left, r0, r1) * units[None])


def couple_pair(coefs, coords):
    u, v = features(coords, 0)
    lower = lower_lanes(v.shape)
    v_two = jnp.concatenate([jnp.where(lower, v, 0.0), jnp.where(lower, 0.0, v)], axis=0)
    columns = jnp.transpose(u)
    u_two = jnp.concatenate([columns[K:], columns[:K]], axis=1)
    tile_high, tile_low = split2(from_square(dot(u_two.astype(BF16), v_two.astype(BF16))))
    swapped = pltpu.roll(coefs, K, 1)
    both = dot3(jnp.concatenate([swapped[:, :K], coefs[:, :K]], axis=0), tile_high, tile_low)
    return jnp.where(lower_lanes((R, 128)), both[:R], both[R:])


def block_diagonal(x):
    leaf = lax.broadcasted_iota(jnp.int32, x.shape, 1) // PT
    wide = x.astype(F32)
    return jnp.concatenate(
        [jnp.where(leaf == k, wide, 0.0) for k in range(GRP)], axis=0
    ).astype(BF16)


def kernel(
    nl, ns,
    charges, points, basis_hbm, transfer, near_list, coupling_list,
    out_hbm,
    basis, out, p8, xe, oe, ua, va, vb, xd, inner0, cross0, inner1, cross1, weight,
    centers, radii, pairs, pair_co, sib,
    up_pair, v_all, c_all, lc,
    send_coef, halo_coef, send_shape, halo_shape,
    root, got_sub, root_b, got_leaf, path_pair, path_co, d1,
    near_send, near_recv, coup_send, coup_recv, sub_send, sub_recv, leaf_send, leaf_recv, local_sem, out_sem,
):
    leaf_id, sub_id = lax.axis_index("leaf"), lax.axis_index("sub")
    count = nl * ns
    me = leaf_id * ns + sub_id
    right, left = lax.rem(me + 1, count), lax.rem(me + count - 1, count)
    left_dev = (left // ns, lax.rem(left, ns))
    right_dev = (right // ns, lax.rem(right, ns))
    sub_devs = [(leaf_id, lax.rem(sub_id + o, ns)) for o in range(1, ns)]
    leaf_devs = [(lax.rem(leaf_id + o, nl), sub_id) for o in range(1, nl)]
    barrier = pltpu.get_barrier_semaphore()
    partners = [left_dev, right_dev] + sub_devs + leaf_devs
    for device in partners:
        pl.semaphore_signal(barrier, inc=1, device_id=device, device_id_type=MESH)

    def send(src, dst, send_sem, recv_sem, device):
        copy = pltpu.make_async_remote_copy(
            src_ref=src, dst_ref=dst, send_sem=send_sem, recv_sem=recv_sem,
            device_id=device, device_id_type=MESH,
        )
        copy.start()
        return copy

    own_charges = pltpu.make_async_copy(
        charges, xe.at[:, pl.ds(GW, LD * PT)], local_sem.at[0]
    )
    own_charges.start()
    own_basis = pltpu.make_async_copy(basis_hbm, basis, local_sem.at[1])
    own_basis.start()
    first = me * LD
    units = unit_rows()
    lane_half = lower_lanes((R, 128))

    p8[3:8, GW : EXT - GW] = jnp.zeros((5, LD * PT), F32)
    p8[0:3, GW : EXT - GW] = points[...]

    own_charges.wait()
    pl.semaphore_wait(barrier, len(partners))
    copies = []
    copies.append(send(xe.at[:, pl.ds(GW, GW)], xe.at[:, pl.ds(EXT - GW, GW)],
                       near_send.at[0], near_recv.at[0], left_dev))
    copies.append(send(xe.at[:, pl.ds(EXT - 2 * GW, GW)], xe.at[:, pl.ds(0, GW)],
                       near_send.at[1], near_recv.at[1], right_dev))
    copies.append(send(p8.at[:, pl.ds(GW, GW)], p8.at[:, pl.ds(EXT - GW, GW)],
                       near_send.at[2], near_recv.at[2], left_dev))
    copies.append(send(p8.at[:, pl.ds(EXT - 2 * GW, GW)], p8.at[:, pl.ds(0, GW)],
                       near_send.at[3], near_recv.at[3], right_dev))
    near_copies = copies

    @pl.loop(0, LD // 32)
    def _(block):
        start = pl.multiple_of(GW + block * (32 * PT), GW)
        wide = p8[:, pl.ds(start, 32 * PT)]
        pts = jnp.stack([wide[:, c * PT : (c + 1) * PT] for c in range(32)])
        rows = pl.ds(block * 32, 32)
        center = jnp.mean(pts, axis=2, keepdims=True)
        off = pts - center
        far = jnp.max(jnp.sum(off * off, axis=1, keepdims=True), axis=2, keepdims=True)
        centers[rows] = jnp.broadcast_to(center, pts.shape)
        radii[rows] = jnp.broadcast_to(jnp.sqrt(far), pts.shape)

    row8 = lax.broadcasted_iota(jnp.int32, (8, 128), 0)
    lane8 = lax.broadcasted_iota(jnp.int32, (8, 128), 1)

    packed_cen, packed_rad = centers[0], radii[0]
    for c in range(1, LD):
        packed_cen = jnp.where(lane8 == c, centers[c], packed_cen)
        packed_rad = jnp.where(lane8 == c, radii[c], packed_rad)
    send_shape[0:8, :] = packed_cen
    send_shape[8:16, :] = packed_rad

    own_basis.wait()

    @pl.loop(0, LD // 32)
    def _(block):
        for s in range(16):
            m = block * 16 + s
            x = xe[:, pl.ds(pl.multiple_of(GW + m * 256, 256), 256)]
            stacked = jnp.concatenate([x[:, :128], x[:, 128:]], axis=0)
            both = basis[pl.ds(2 * m, 2)].reshape(2 * K, PT)
            product = dot_nt(stacked, both)
            pair = jnp.where(lane_half, product[:R], product[R:])
            pairs[m] = pair
            send_coef[m] = pair.astype(BF16)

    half_pairs = REACH // 2
    coup_copies = [
        send(send_coef.at[pl.ds(0, half_pairs)], halo_coef.at[1],
             coup_send.at[0], coup_recv.at[0], left_dev),
        send(send_coef.at[pl.ds(half_pairs, half_pairs)], halo_coef.at[0],
             coup_send.at[1], coup_recv.at[1], right_dev),
        send(send_shape, halo_shape.at[1], coup_send.at[2], coup_recv.at[2], left_dev),
        send(send_shape, halo_shape.at[0], coup_send.at[3], coup_recv.at[3], right_dev),
    ]

    t0, t1 = transfer[0], transfer[1]
    up = jnp.concatenate([t0, t1], axis=0)
    up_high, up_low = split2(jnp.concatenate([up, up], axis=1))
    down = jnp.concatenate([jnp.transpose(t0), jnp.transpose(t1)], axis=1)
    down_high, down_low = split2(jnp.concatenate([down, down], axis=0))

    def lift(pair_block):
        n = pair_block.shape[0]
        return dot3(pair_block.reshape(n * R, 128), up_high, up_low).reshape(n, R, 128)

    level_cen, level_rad = centers[...], radii[...]
    offset, n = 0, LD // 2
    block = None
    while n > 1:
        level_cen, level_rad = merge_shapes(level_cen, level_rad)
        if n >= 32:

            def lift_part(i, offset=offset, n=n):
                some = pairs[pl.ds(offset + i * 16, 16)]
                pairs[pl.ds(offset + n + i * 8, 8)] = side_by_side(lift(some))

            pl.loop(0, n // 16)(lift_part)
        else:
            if block is None:
                block = pairs[pl.ds(offset, n)]
            block = side_by_side(lift(block))
            pairs[pl.ds(offset + n, n // 2)] = block
        offset += n
        n //= 2
        pair_co[pl.ds(offset - LD // 2, n)] = pair_coords(level_cen, level_rad, units)
    root_coef = lift(block)[0]
    root_cen, root_rad = merge_shapes(level_cen, level_rad)

    def packed_shape(cen, rad):
        return jnp.where(row8 < 3, cen, rad)

    def unpacked_shape(shape):
        rows = lax.broadcasted_iota(jnp.int32, shape.shape, 1)
        cen = jnp.where(rows < 3, shape, 0.0)
        rad = jnp.sum(jnp.where(rows == 3, shape, 0.0), axis=1, keepdims=True)
        return cen, jnp.broadcast_to(rad, shape.shape)

    root[0:R, :] = root_coef
    root[R : R + 8, :] = packed_shape(root_cen[0], root_rad[0])
    sub_copies = [
        send(root, got_sub.at[sub_id], sub_send.at[o], sub_recv.at[o], device)
        for o, device in enumerate(sub_devs)
    ]
    got_sub[sub_id] = root[...]

    leaf_lane = lax.broadcasted_iota(jnp.int32, (8, LD), 1)
    base = first + (leaf_lane // GRP) * GRP - GRP
    listed_leaf = near_list[...]
    relative = jnp.where(listed_leaf >= 0, listed_leaf - base, -1)
    slot_row = lax.broadcasted_iota(jnp.int32, (16, LD), 0)
    counts = jnp.zeros((16, LD), F32)
    for k in range(3 * GRP):
        times = jnp.sum(jnp.where(relative == k, 1.0, 0.0), axis=0, keepdims=True)
        counts = jnp.where(slot_row == k, times, counts)
    columns = jnp.transpose(counts).astype(BF16)
    for k in range(3 * GRP):
        ones = jnp.where(slot_row == k, 1.0, 0.0).astype(BF16)
        weight[k, 0:8, :] = jnp.zeros((8, 128), F32)
        weight[k, 8 : 8 + LD, :] = dot(columns, ones)
        weight[k, 8 + LD : 16 + LD, :] = jnp.zeros((8, 128), F32)

    for copy in near_copies:
        copy.wait()

    def near_features(g):
        lanes = pl.ds(pl.multiple_of(g * GW, GW), GW)
        row = lax.broadcasted_iota(jnp.int32, (8, GW), 0)
        z0 = lax.convert_element_type(me * GROUPS + g - 1, F32)
        corner = jnp.where(row == 2, z0, jnp.where(row < 2, 1.0, 0.0))
        low = p8[:, lanes] - corner
        shift = jnp.where(row == 2, 1.0, 0.0)
        u, v = features(SCALE * (low - shift), 0)
        ua[:, lanes] = u.astype(BF16)
        va[:, lanes] = v.astype(BF16)
        vb[:, lanes] = features(SCALE * low, 0)[1].astype(BF16)
        xd[pl.ds(pl.multiple_of(g * 128, 128), 128), :] = block_diagonal(xe[:, lanes])

    oe[:, 0:GW] = jnp.zeros((R, GW), F32)

    def near_tiles(g, inner, cross):
        here = pl.ds(pl.multiple_of(g * GW, GW), GW)
        there = pl.ds(pl.multiple_of(g * GW + GW, GW), GW)
        u, v, v_next = ua[:, here], va[:, here], vb[:, there]
        for i in range(GRP):
            rows = slice(i * PT, (i + 1) * PT)
            inner[rows, i * PT :] = from_square(dot_tn(u[:, rows], v[:, i * PT :])).astype(BF16)
            cross[rows, :] = from_square(dot_tn(u[:, rows], v_next)).astype(BF16)

    def near_sums(g, inner, cross):
        here = pl.ds(pl.multiple_of(g * GW, GW), GW)
        there = pl.ds(pl.multiple_of(g * GW + GW, GW), GW)

        def times(k, target):
            return weight[k, pl.ds(g * GRP + target + GRP, 1), :]

        def part(block, source, target=0):
            return block[source * R : (source + 1) * R, target * PT : (target + 1) * PT]

        x = xd[pl.ds(pl.multiple_of(g * 128, 128), 128), :]
        x_next = xd[pl.ds(pl.multiple_of(g * 128 + 128, 128), 128), :]
        own = [part(oe[:, here], 0, j) for j in range(GRP)]
        nugget = xe[:, there].astype(F32)
        following = [part(nugget, 0, j) for j in range(GRP)]
        for c in range(0, GRP, 2):
            n = c + 2
            to_later = dot(x[: n * R, : n * PT], inner[: n * PT, c * PT : n * PT])
            for j in range(c, n):
                for i in range(j + 1):
                    own[j] = own[j] + times(GRP + i, j) * part(to_later, i, j - c)
        for i in range(GRP - 1):
            n = i + 1
            to_earlier = dot_nt(x[n * R :, n * PT :], inner[i * PT : n * PT, n * PT :])
            for j in range(n, GRP):
                own[i] = own[i] + times(GRP + j, i) * part(to_earlier, j - n)
        forth, back = dot(x, cross[...]), dot_nt(x_next, cross[...])
        for j in range(GRP):
            for i in range(GRP):
                following[j] = following[j] + times(i, GRP + j) * part(forth, i, j)
                own[i] = own[i] + times(2 * GRP + j, i) * part(back, j, i)
        oe[:, here] = jnp.concatenate(own, axis=1)
        oe[:, there] = jnp.concatenate(following, axis=1)

    middle_row = lax.broadcasted_iota(jnp.int32, (1, 8, 128), 1)
    middle = jnp.where(
        middle_row == 2,
        (me * GROUPS + GROUPS // 2).astype(F32),
        jnp.where(middle_row < 2, 1.0, 0.0),
    )

    def put_leaves(where, cen, rad):
        u, v = features(SCALE * (cen - middle + rad * units[None]), 1)
        v_all[pl.ds(where, 8)] = v.astype(BF16)
        return u

    def put_coefs(where, two):
        other = pltpu.roll(two, K, 1)
        c_all[where] = jnp.where(lane_half, two, other).astype(BF16)
        c_all[where + 1] = jnp.where(lane_half, other, two).astype(BF16)

    def coupling_own(b):
        u = put_leaves(REACH + b * 8, centers[pl.ds(b * 8, 8)], radii[pl.ds(b * 8, 8)])
        up_pair[pl.ds(b * 4, 4)] = side_by_side(u).astype(BF16)
        for s in range(4):
            put_coefs(REACH + b * 8 + 2 * s, pairs[b * 4 + s])

    def coupling_halo(side, b):
        start = side * (REACH + LD) + b * 8
        turn = lax.rem(LD + (1 - side) * REACH - b * 8, LD)
        shape = pltpu.roll(halo_shape[side], turn, 1)
        cens = [jnp.broadcast_to(shape[0:8, s : s + 1], (8, 128)) for s in range(8)]
        rads = [jnp.broadcast_to(shape[8:16, s : s + 1], (8, 128)) for s in range(8)]
        put_leaves(start, jnp.stack(cens), jnp.stack(rads))
        for s in range(4):
            put_coefs(start + 2 * s, halo_coef[side, b * 4 + s].astype(F32))

    def siblings(b):
        for s in range(4):
            i = jnp.minimum(b * 4 + s, LD // 2 - 2)
            sib[i] = couple_pair(pairs[LD // 2 + i], pair_co[i])

    for g in range(4):
        near_features(g)
    for inner in (inner0, inner1):
        for c in (0, 2):
            inner[(c + 1) * PT : (c + 2) * PT, c * PT : (c + 1) * PT] = jnp.zeros((PT, PT), BF16)
    near_tiles(0, inner0, cross0)

    def near_turn(h):
        near_tiles(2 * h + 1, inner1, cross1)
        near_sums(2 * h, inner0, cross0)
        near_tiles(2 * h + 2, inner0, cross0)
        near_sums(2 * h + 1, inner1, cross1)
        for s in range(2):
            near_features(jnp.minimum(2 * h + 4 + s, GROUPS + 1))
        siblings(h)

    @pl.loop(0, GROUPS // 4)
    def _(h):
        near_turn(h)
        coupling_own(2 * h)
        coupling_own(2 * h + 1)

    for copy in coup_copies:
        copy.wait()

    @pl.loop(0, GROUPS // 4)
    def _(h):
        near_turn(GROUPS // 4 + h)
        coupling_halo(0, h)
        coupling_halo(1, h)

    near_sums(GROUPS, inner0, cross0)

    def climb(got, width, level0, index):
        coefs = got[:, 0:R, :]
        cen, rad = unpacked_shape(got[:, R : R + 8, :])
        level = level0
        while width > 1:
            two = side_by_side(coefs)
            path_pair[level, pl.ds(0, width // 2)] = two
            path_co[level, pl.ds(0, width // 2)] = pair_coords(cen, rad, units)
            coefs = lift(two)
            cen, rad = merge_shapes(cen, rad)
            width //= 2
            level += 1
        return coefs[0], packed_shape(cen[0], rad[0])

    sub_levels, leaf_levels = ns.bit_length() - 1, nl.bit_length() - 1
    for copy in sub_copies:
        copy.wait()
    top_coef, top_shape = climb(got_sub[...], ns, 0, sub_id)
    root_b[0:R, :] = top_coef
    root_b[R : R + 8, :] = top_shape
    leaf_copies = [
        send(root_b, got_leaf.at[leaf_id], leaf_send.at[o], leaf_recv.at[o], device)
        for o, device in enumerate(leaf_devs)
    ]
    got_leaf[leaf_id] = root_b[...]

    dead = LD + 2 * REACH
    for ref in (c_all, v_all):
        ref[dead] = jnp.zeros(ref.shape[1:], BF16)
    first_half = lower_lanes((FEAT, 128))

    def listed(m):
        u = jnp.transpose(up_pair[m].astype(F32)).astype(BF16)
        tiles, sources = [], []
        for s in range(2):
            leaf = 2 * m + s
            vs, cs = [], []
            for t in range(4):
                picked = []
                for slot in (2 * t, 2 * t + 1):
                    j = coupling_list[slot, leaf]
                    near_by = jnp.clip(j - first + REACH, 0, dead - 1)
                    picked.append(jnp.where(j >= 0, near_by, dead))
                vs.append(jnp.where(first_half, v_all[picked[0]], v_all[picked[1]]))
                cs.append(jnp.where(first_half, c_all[picked[0]], c_all[picked[1]]))
            d2 = dot(u[s * K : (s + 1) * K], jnp.concatenate(vs, axis=1))
            tiles.append(from_square(d2).astype(BF16))
            sources.append(jnp.concatenate(cs, axis=1))
        return jnp.concatenate(sources, axis=0), jnp.concatenate(tiles, axis=0)

    def couple_four(b):
        operands = [listed(b * 4 + s) for s in range(4)]
        for s in range(4):
            product = dot_nt(*operands[s])
            lc[b * 4 + s] = jnp.where(lane_half, product[:R], product[R:])

    beside = 4
    pl.loop(0, LD // 8 - beside)(couple_four)

    for copy in leaf_copies:
        copy.wait()
    climb(got_leaf[...], nl, sub_levels, leaf_id)

    def masked(pair, side):
        chosen = lower_lanes(pair.shape) == (side == 0)
        return jnp.where(chosen, pair, 0.0)

    held = None
    for level in reversed(range(sub_levels + leaf_levels)):
        position = (sub_id if level < sub_levels else leaf_id)
        shift = level if level < sub_levels else level - sub_levels
        node = position // (2**shift)
        pair = node // 2
        mine = couple_pair(path_pair[level, pair], path_co[level, pair])
        if held is not None:
            mine = mine + dot3(held, down_high, down_low)
        held = masked(mine, lax.rem(node, 2))

    def spread(pair_block):
        n = pair_block.shape[0]
        lower = lower_lanes(pair_block.shape)
        both = jnp.stack(
            [jnp.where(lower, pair_block, 0.0), jnp.where(lower, 0.0, pair_block)], axis=1
        )
        return dot3(both.reshape(2 * n * R, 128), down_high, down_low).reshape(2 * n, R, 128)

    n, offset = 1, LD // 2 - 2
    block = sib[pl.ds(offset, 1)] + dot3(held, down_high, down_low)[None]
    while n < LD // 4:
        block = spread(block)
        n *= 2
        offset -= n
        block = block + sib[pl.ds(offset, n)]
    d1[...] = block
    for b in range(LD // 8 - beside, LD // 8):
        couple_four(b)

    def put_out(b):
        lanes = pl.ds(pl.multiple_of(b * 32 * PT, 32 * PT), 32 * PT)
        return pltpu.make_async_copy(out.at[:, lanes], out_hbm.at[:, lanes], out_sem.at[b])

    @pl.loop(0, LD // 32)
    def _(b):
        below = spread(d1[pl.ds(b * 8, 8)])
        for s in range(16):
            m = b * 16 + s
            coef = lc[m] + below[s]
            stacked = jnp.concatenate(
                [jnp.where(lane_half, coef, 0.0), jnp.where(lane_half, 0.0, coef)], axis=0
            ).astype(BF16)
            far = dot(stacked, basis[pl.ds(2 * m, 2)].reshape(2 * K, PT))
            start = pl.multiple_of(m * 256, 256)
            near = oe[:, pl.ds(pl.multiple_of(GW + m * 256, 256), 256)]
            out[:, pl.ds(start, 256)] = near + jnp.concatenate([far[:R], far[R:]], axis=1)
        put_out(b).start()

    for b in range(LD // 32):
        put_out(b).wait()


def per_device(charges, points, basis, transfer, near_list, coupling_list):
    nl, ns = lax.axis_size("leaf"), lax.axis_size("sub")
    levels = (nl * ns).bit_length() - 1
    widest = max(nl, ns) // 2
    vmem = pl.BlockSpec(memory_space=pltpu.VMEM)
    hbm = pl.BlockSpec(memory_space=pl.ANY)
    total = LD + 2 * REACH + 1

    def body(*refs):
        kernel(nl, ns, *refs)

    dma = pltpu.SemaphoreType.DMA
    return pl.pallas_call(
        body,
        out_shape=jax.ShapeDtypeStruct((R, LD * PT), F32),
        in_specs=[hbm, vmem, hbm, vmem, vmem, pl.BlockSpec(memory_space=pltpu.SMEM)],
        out_specs=hbm,
        scratch_shapes=[
            pltpu.VMEM((LD, K, PT), BF16),
            pltpu.VMEM((R, LD * PT), F32),
            pltpu.VMEM((8, EXT), F32),
            pltpu.VMEM((R, EXT), BF16),
            pltpu.VMEM((R, EXT), F32),
            pltpu.VMEM((FEAT, EXT), BF16),
            pltpu.VMEM((FEAT, EXT), BF16),
            pltpu.VMEM((FEAT, EXT), BF16),
            pltpu.VMEM(((GROUPS + 2) * 128, GW), BF16),
            pltpu.VMEM((GW, GW), BF16),
            pltpu.VMEM((GW, GW), BF16),
            pltpu.VMEM((GW, GW), BF16),
            pltpu.VMEM((GW, GW), BF16),
            pltpu.VMEM((3 * GRP, LD + 16, 128), F32),
            pltpu.VMEM((LD, 8, 128), F32),
            pltpu.VMEM((LD, 8, 128), F32),
            pltpu.VMEM((LD, R, 128), F32),
            pltpu.VMEM((LD // 2, 8, 128), F32),
            pltpu.VMEM((LD // 2, R, 128), F32),
            pltpu.VMEM((LD // 2, FEAT, 128), BF16),
            pltpu.VMEM((total, FEAT, 128), BF16),
            pltpu.VMEM((total, R, 128), BF16),
            pltpu.VMEM((LD // 2, R, 128), F32),
            pltpu.VMEM((LD // 2, R, 128), BF16),
            pltpu.VMEM((2, REACH // 2, R, 128), BF16),
            pltpu.VMEM((16, 128), F32),
            pltpu.VMEM((2, 16, 128), F32),
            pltpu.VMEM((R + 8, 128), F32),
            pltpu.VMEM((ns, R + 8, 128), F32),
            pltpu.VMEM((R + 8, 128), F32),
            pltpu.VMEM((nl, R + 8, 128), F32),
            pltpu.VMEM((levels, widest, R, 128), F32),
            pltpu.VMEM((levels, widest, 8, 128), F32),
            pltpu.VMEM((LD // 4, R, 128), F32),
            dma((4,)), dma((4,)), dma((4,)), dma((4,)),
            dma((ns,)), dma((ns,)), dma((nl,)), dma((nl,)), dma((2,)), dma((LD // 32,)),
        ],
        compiler_params=pltpu.CompilerParams(
            collective_id=0, has_side_effects=True, vmem_limit_bytes=56 * 2**20
        ),
        cost_estimate=pl.CostEstimate(
            flops=6 * 10**9, bytes_accessed=7 * 10**6, transcendentals=4 * 10**7
        ),
    )(charges, points, basis, transfer, near_list.T, coupling_list.T)


def solution(mesh):
    in_specs = (
        P(None, ("leaf", "sub")),
        P(None, ("leaf", "sub")),
        P(("leaf", "sub"), None, None),
        P(),
        P(("leaf", "sub"), None),
        P(("leaf", "sub"), None),
    )
    return jax.shard_map(
        per_device,
        mesh=mesh,
        in_specs=in_specs,
        out_specs=P(None, ("leaf", "sub")),
        check_vma=False,
    )
```

```python
import math

import jax
import jax.numpy as jnp
from jax import lax
from jax.experimental import pallas as pl
from jax.experimental.pallas import tpu as pltpu
from jax.sharding import PartitionSpec as P

F32, BF16 = jnp.float32, jnp.bfloat16
PT = 128
K = 64
R = 32
LD = 128
REACH = 64
GRP = 4
GW = GRP * PT
GROUPS = LD // GRP
EXT = (GROUPS + 2) * GW
FEAT = 32
SCALE = math.log2(math.e) / 2.0
TINY = 1e-30
MESH = pl.DeviceIdType.MESH


def dot(a, b):
    return lax.dot_general(a, b, (((1,), (0,)), ((), ())), preferred_element_type=F32)


def dot_nt(a, b):
    return lax.dot_general(a, b, (((1,), (1,)), ((), ())), preferred_element_type=F32)


def dot_tn(a, b):
    return lax.dot_general(a, b, (((0,), (0,)), ((), ())), preferred_element_type=F32)


def split2(x):
    high = x.astype(BF16)
    return high, (x - high.astype(F32)).astype(BF16)


def dot3(a, b_high, b_low):
    high, low = split2(a)
    n = a.shape[0]
    both = dot(jnp.concatenate([high, low], axis=0), b_high)
    return both[:n] + (dot(high, b_low) + both[n:])


def from_square(d2):
    x = jnp.maximum(d2, TINY)
    return jnp.exp2(-(x * lax.rsqrt(x)))


def features(coords, axis):
    high = coords.astype(BF16).astype(F32)
    low = (coords - high).astype(BF16).astype(F32)
    kept = high + low
    norm = jnp.sum(kept * kept, axis=axis, keepdims=True)
    n1 = norm.astype(BF16).astype(F32)
    n2 = (norm - n1).astype(BF16).astype(F32)
    n3 = norm - n1 - n2
    row = lax.broadcasted_iota(jnp.int32, coords.shape, axis)
    ones = jnp.where((row >= 4) & (row < 7), 1.0, 0.0)
    norms = jnp.where(row == 0, n1, jnp.where(row == 1, n2, jnp.where(row == 2, n3, ones)))
    both = high + pltpu.roll(low, 4, axis)
    twice = -2.0 * both
    zero = jnp.zeros_like(both)
    u = jnp.concatenate([both, both, norms, zero], axis=axis)
    v = jnp.concatenate(
        [twice, pltpu.roll(twice, 4, axis), pltpu.roll(norms, 4, axis), zero], axis=axis
    )
    return u, v


def unit_rows():
    row = lax.broadcasted_iota(jnp.int32, (8, 128), 0)
    index = lax.broadcasted_iota(jnp.int32, (8, 128), 1) % K
    digit = jnp.where(row == 0, index // 16, jnp.where(row == 1, index // 4 % 4, index % 4))
    big, small = math.cos(math.pi / 8.0), math.cos(3.0 * math.pi / 8.0)
    value = jnp.where(
        digit == 0, big, jnp.where(digit == 1, small, jnp.where(digit == 2, -small, -big))
    )
    return jnp.where(row < 3, value, 0.0).astype(F32)


def lower_lanes(shape):
    return lax.broadcasted_iota(jnp.int32, shape, len(shape) - 1) < K


def halves(x):
    paired = x.reshape((x.shape[0] // 2, 2) + x.shape[1:])
    return paired[:, 0], paired[:, 1]


def side_by_side(x):
    left, right = halves(x)
    return jnp.where(lower_lanes(left.shape), left, right)


def merge_shapes(centers, radii):
    c0, c1 = halves(centers)
    r0, r1 = halves(radii)
    gap = c0 - c1
    reach = jnp.sqrt(jnp.sum(gap * gap, axis=1, keepdims=True))
    return 0.5 * (c0 + c1), jnp.maximum(r0, r1) + 0.5 * reach


def pair_coords(centers, radii, units):
    c0, c1 = halves(centers)
    r0, r1 = halves(radii)
    half = 0.5 * (c0 - c1)
    left = lower_lanes(half.shape)
    return SCALE * (jnp.where(left, half, -half) + jnp.where(left, r0, r1) * units[None])


def couple_pair(coefs, coords):
    u, v = features(coords, 0)
    lower = lower_lanes(v.shape)
    v_two = jnp.concatenate([jnp.where(lower, v, 0.0), jnp.where(lower, 0.0, v)], axis=0)
    columns = jnp.transpose(u)
    u_two = jnp.concatenate([columns[K:], columns[:K]], axis=1)
    tile_high, tile_low = split2(from_square(dot(u_two.astype(BF16), v_two.astype(BF16))))
    swapped = pltpu.roll(coefs, K, 1)
    both = dot3(jnp.concatenate([swapped[:, :K], coefs[:, :K]], axis=0), tile_high, tile_low)
    return jnp.where(lower_lanes((R, 128)), both[:R], both[R:])


def block_diagonal(x):
    leaf = lax.broadcasted_iota(jnp.int32, x.shape, 1) // PT
    wide = x.astype(F32)
    return jnp.concatenate(
        [jnp.where(leaf == k, wide, 0.0) for k in range(GRP)], axis=0
    ).astype(BF16)


def kernel(
    nl, ns,
    charges, points, basis_hbm, transfer, near_list, coupling_list,
    out_hbm,
    basis, out, p8, xe, oe, ua, va, vb, xd, inner0, cross0, inner1, cross1, weight,
    centers, radii, pairs, pair_co, sib,
    up_pair, v_all, c_all, lc,
    send_coef, halo_coef, send_shape, halo_shape,
    root, got_sub, root_b, got_leaf, path_pair, path_co, d1,
    near_send, near_recv, coup_send, coup_recv, sub_send, sub_recv, leaf_send, leaf_recv, local_sem, out_sem,
):
    leaf_id, sub_id = lax.axis_index("leaf"), lax.axis_index("sub")
    count = nl * ns
    me = leaf_id * ns + sub_id
    right, left = lax.rem(me + 1, count), lax.rem(me + count - 1, count)
    left_dev = (left // ns, lax.rem(left, ns))
    right_dev = (right // ns, lax.rem(right, ns))
    sub_devs = [(leaf_id, lax.rem(sub_id + o, ns)) for o in range(1, ns)]
    leaf_devs = [(lax.rem(leaf_id + o, nl), sub_id) for o in range(1, nl)]
    barrier = pltpu.get_barrier_semaphore()
    partners = [left_dev, right_dev] + sub_devs + leaf_devs
    for device in partners:
        pl.semaphore_signal(barrier, inc=1, device_id=device, device_id_type=MESH)

    def send(src, dst, send_sem, recv_sem, device):
        copy = pltpu.make_async_remote_copy(
            src_ref=src, dst_ref=dst, send_sem=send_sem, recv_sem=recv_sem,
            device_id=device, device_id_type=MESH,
        )
        copy.start()
        return copy

    own_charges = pltpu.make_async_copy(
        charges, xe.at[:, pl.ds(GW, LD * PT)], local_sem.at[0]
    )
    own_charges.start()
    own_basis = pltpu.make_async_copy(basis_hbm, basis, local_sem.at[1])
    own_basis.start()
    first = me * LD
    units = unit_rows()
    lane_half = lower_lanes((R, 128))

    p8[3:8, GW : EXT - GW] = jnp.zeros((5, LD * PT), F32)
    p8[0:3, GW : EXT - GW] = points[...]

    own_charges.wait()
    pl.semaphore_wait(barrier, len(partners))
    copies = []
    copies.append(send(xe.at[:, pl.ds(GW, GW)], xe.at[:, pl.ds(EXT - GW, GW)],
                       near_send.at[0], near_recv.at[0], left_dev))
    copies.append(send(xe.at[:, pl.ds(EXT - 2 * GW, GW)], xe.at[:, pl.ds(0, GW)],
                       near_send.at[1], near_recv.at[1], right_dev))
    copies.append(send(p8.at[:, pl.ds(GW, GW)], p8.at[:, pl.ds(EXT - GW, GW)],
                       near_send.at[2], near_recv.at[2], left_dev))
    copies.append(send(p8.at[:, pl.ds(EXT - 2 * GW, GW)], p8.at[:, pl.ds(0, GW)],
                       near_send.at[3], near_recv.at[3], right_dev))
    near_copies = copies

    @pl.loop(0, LD // 32)
    def _(block):
        start = pl.multiple_of(GW + block * (32 * PT), GW)
        wide = p8[:, pl.ds(start, 32 * PT)]
        pts = jnp.stack([wide[:, c * PT : (c + 1) * PT] for c in range(32)])
        rows = pl.ds(block * 32, 32)
        center = jnp.mean(pts, axis=2, keepdims=True)
        off = pts - center
        far = jnp.max(jnp.sum(off * off, axis=1, keepdims=True), axis=2, keepdims=True)
        centers[rows] = jnp.broadcast_to(center, pts.shape)
        radii[rows] = jnp.broadcast_to(jnp.sqrt(far), pts.shape)

    row8 = lax.broadcasted_iota(jnp.int32, (8, 128), 0)
    lane8 = lax.broadcasted_iota(jnp.int32, (8, 128), 1)

    packed_cen, packed_rad = centers[0], radii[0]
    for c in range(1, LD):
        packed_cen = jnp.where(lane8 == c, centers[c], packed_cen)
        packed_rad = jnp.where(lane8 == c, radii[c], packed_rad)
    send_shape[0:8, :] = packed_cen
    send_shape[8:16, :] = packed_rad

    own_basis.wait()

    @pl.loop(0, LD // 32)
    def _(block):
        for s in range(16):
            m = block * 16 + s
            x = xe[:, pl.ds(pl.multiple_of(GW + m * 256, 256), 256)]
            stacked = jnp.concatenate([x[:, :128], x[:, 128:]], axis=0)
            both = basis[pl.ds(2 * m, 2)].reshape(2 * K, PT)
            product = dot_nt(stacked, both)
            pair = jnp.where(lane_half, product[:R], product[R:])
            pairs[m] = pair
            send_coef[m] = pair.astype(BF16)

    half_pairs = REACH // 2
    coup_copies = [
        send(send_coef.at[pl.ds(0, half_pairs)], halo_coef.at[1],
             coup_send.at[0], coup_recv.at[0], left_dev),
        send(send_coef.at[pl.ds(half_pairs, half_pairs)], halo_coef.at[0],
             coup_send.at[1], coup_recv.at[1], right_dev),
        send(send_shape, halo_shape.at[1], coup_send.at[2], coup_recv.at[2], left_dev),
        send(send_shape, halo_shape.at[0], coup_send.at[3], coup_recv.at[3], right_dev),
    ]

    t0, t1 = transfer[0], transfer[1]
    up = jnp.concatenate([t0, t1], axis=0)
    up_high, up_low = split2(jnp.concatenate([up, up], axis=1))
    down = jnp.concatenate([jnp.transpose(t0), jnp.transpose(t1)], axis=1)
    down_high, down_low = split2(jnp.concatenate([down, down], axis=0))

    def lift(pair_block):
        n = pair_block.shape[0]
        return dot3(pair_block.reshape(n * R, 128), up_high, up_low).reshape(n, R, 128)

    level_cen, level_rad = centers[...], radii[...]
    offset, n = 0, LD // 2
    block = None
    while n > 1:
        level_cen, level_rad = merge_shapes(level_cen, level_rad)
        if n >= 32:

            def lift_part(i, offset=offset, n=n):
                some = pairs[pl.ds(offset + i * 16, 16)]
                pairs[pl.ds(offset + n + i * 8, 8)] = side_by_side(lift(some))

            pl.loop(0, n // 16)(lift_part)
        else:
            if block is None:
                block = pairs[pl.ds(offset, n)]
            block = side_by_side(lift(block))
            pairs[pl.ds(offset + n, n // 2)] = block
        offset += n
        n //= 2
        pair_co[pl.ds(offset - LD // 2, n)] = pair_coords(level_cen, level_rad, units)
    root_coef = lift(block)[0]
    root_cen, root_rad = merge_shapes(level_cen, level_rad)

    def packed_shape(cen, rad):
        return jnp.where(row8 < 3, cen, rad)

    def unpacked_shape(shape):
        rows = lax.broadcasted_iota(jnp.int32, shape.shape, 1)
        cen = jnp.where(rows < 3, shape, 0.0)
        rad = jnp.sum(jnp.where(rows == 3, shape, 0.0), axis=1, keepdims=True)
        return cen, jnp.broadcast_to(rad, shape.shape)

    root[0:R, :] = root_coef
    root[R : R + 8, :] = packed_shape(root_cen[0], root_rad[0])
    sub_copies = [
        send(root, got_sub.at[sub_id], sub_send.at[o], sub_recv.at[o], device)
        for o, device in enumerate(sub_devs)
    ]
    got_sub[sub_id] = root[...]

    leaf_lane = lax.broadcasted_iota(jnp.int32, (8, LD), 1)
    base = first + (leaf_lane // GRP) * GRP - GRP
    listed_leaf = near_list[...]
    relative = jnp.where(listed_leaf >= 0, listed_leaf - base, -1)
    slot_row = lax.broadcasted_iota(jnp.int32, (16, LD), 0)
    counts = jnp.zeros((16, LD), F32)
    for k in range(3 * GRP):
        times = jnp.sum(jnp.where(relative == k, 1.0, 0.0), axis=0, keepdims=True)
        counts = jnp.where(slot_row == k, times, counts)
    columns = jnp.transpose(counts).astype(BF16)
    for k in range(3 * GRP):
        ones = jnp.where(slot_row == k, 1.0, 0.0).astype(BF16)
        weight[k, 0:8, :] = jnp.zeros((8, 128), F32)
        weight[k, 8 : 8 + LD, :] = dot(columns, ones)
        weight[k, 8 + LD : 16 + LD, :] = jnp.zeros((8, 128), F32)

    for copy in near_copies:
        copy.wait()

    def near_features(g):
        lanes = pl.ds(pl.multiple_of(g * GW, GW), GW)
        row = lax.broadcasted_iota(jnp.int32, (8, GW), 0)
        z0 = lax.convert_element_type(me * GROUPS + g - 1, F32)
        corner = jnp.where(row == 2, z0, jnp.where(row < 2, 1.0, 0.0))
        low = p8[:, lanes] - corner
        shift = jnp.where(row == 2, 1.0, 0.0)
        u, v = features(SCALE * (low - shift), 0)
        ua[:, lanes] = u.astype(BF16)
        va[:, lanes] = v.astype(BF16)
        vb[:, lanes] = features(SCALE * low, 0)[1].astype(BF16)
        xd[pl.ds(pl.multiple_of(g * 128, 128), 128), :] = block_diagonal(xe[:, lanes])

    oe[:, 0:GW] = jnp.zeros((R, GW), F32)

    def near_tiles(g, inner, cross):
        here = pl.ds(pl.multiple_of(g * GW, GW), GW)
        there = pl.ds(pl.multiple_of(g * GW + GW, GW), GW)
        u, v, v_next = ua[:, here], va[:, here], vb[:, there]
        for i in range(GRP):
            rows = slice(i * PT, (i + 1) * PT)
            inner[rows, i * PT :] = from_square(dot_tn(u[:, rows], v[:, i * PT :])).astype(BF16)
            cross[rows, :] = from_square(dot_tn(u[:, rows], v_next)).astype(BF16)

    def near_sums(g, inner, cross):
        here = pl.ds(pl.multiple_of(g * GW, GW), GW)
        there = pl.ds(pl.multiple_of(g * GW + GW, GW), GW)

        def times(k, target):
            return weight[k, pl.ds(g * GRP + target + GRP, 1), :]

        def part(block, source, target=0):
            return block[source * R : (source + 1) * R, target * PT : (target + 1) * PT]

        x = xd[pl.ds(pl.multiple_of(g * 128, 128), 128), :]
        x_next = xd[pl.ds(pl.multiple_of(g * 128 + 128, 128), 128), :]
        own = [part(oe[:, here], 0, j) for j in range(GRP)]
        nugget = xe[:, there].astype(F32)
        following = [part(nugget, 0, j) for j in range(GRP)]
        for c in range(0, GRP, 2):
            n = c + 2
            to_later = dot(x[: n * R, : n * PT], inner[: n * PT, c * PT : n * PT])
            for j in range(c, n):
                for i in range(j + 1):
                    own[j] = own[j] + times(GRP + i, j) * part(to_later, i, j - c)
        for i in range(GRP - 1):
            n = i + 1
            to_earlier = dot_nt(x[n * R :, n * PT :], inner[i * PT : n * PT, n * PT :])
            for j in range(n, GRP):
                own[i] = own[i] + times(GRP + j, i) * part(to_earlier, j - n)
        forth, back = dot(x, cross[...]), dot_nt(x_next, cross[...])
        for j in range(GRP):
            for i in range(GRP):
                following[j] = following[j] + times(i, GRP + j) * part(forth, i, j)
                own[i] = own[i] + times(2 * GRP + j, i) * part(back, j, i)
        oe[:, here] = jnp.concatenate(own, axis=1)
        oe[:, there] = jnp.concatenate(following, axis=1)

    middle_row = lax.broadcasted_iota(jnp.int32, (1, 8, 128), 1)
    middle = jnp.where(
        middle_row == 2,
        (me * GROUPS + GROUPS // 2).astype(F32),
        jnp.where(middle_row < 2, 1.0, 0.0),
    )

    def put_leaves(where, cen, rad):
        u, v = features(SCALE * (cen - middle + rad * units[None]), 1)
        v_all[pl.ds(where, 8)] = v.astype(BF16)
        return u

    def put_coefs(where, two):
        other = pltpu.roll(two, K, 1)
        c_all[where] = jnp.where(lane_half, two, other).astype(BF16)
        c_all[where + 1] = jnp.where(lane_half, other, two).astype(BF16)

    def coupling_own(b):
        u = put_leaves(REACH + b * 8, centers[pl.ds(b * 8, 8)], radii[pl.ds(b * 8, 8)])
        up_pair[pl.ds(b * 4, 4)] = side_by_side(u).astype(BF16)
        for s in range(4):
            put_coefs(REACH + b * 8 + 2 * s, pairs[b * 4 + s])

    def coupling_halo(side, b):
        start = side * (REACH + LD) + b * 8
        turn = lax.rem(LD + (1 - side) * REACH - b * 8, LD)
        shape = pltpu.roll(halo_shape[side], turn, 1)
        cens = [jnp.broadcast_to(shape[0:8, s : s + 1], (8, 128)) for s in range(8)]
        rads = [jnp.broadcast_to(shape[8:16, s : s + 1], (8, 128)) for s in range(8)]
        put_leaves(start, jnp.stack(cens), jnp.stack(rads))
        for s in range(4):
            put_coefs(start + 2 * s, halo_coef[side, b * 4 + s].astype(F32))

    def siblings(b):
        for s in range(4):
            i = jnp.minimum(b * 4 + s, LD // 2 - 2)
            sib[i] = couple_pair(pairs[LD // 2 + i], pair_co[i])

    for g in range(4):
        near_features(g)
    for inner in (inner0, inner1):
        for c in (0, 2):
            inner[(c + 1) * PT : (c + 2) * PT, c * PT : (c + 1) * PT] = jnp.zeros((PT, PT), BF16)
    near_tiles(0, inner0, cross0)

    def near_turn(h):
        near_tiles(2 * h + 1, inner1, cross1)
        near_sums(2 * h, inner0, cross0)
        near_tiles(2 * h + 2, inner0, cross0)
        near_sums(2 * h + 1, inner1, cross1)
        for s in range(2):
            near_features(jnp.minimum(2 * h + 4 + s, GROUPS + 1))
        siblings(h)

    @pl.loop(0, GROUPS // 4)
    def _(h):
        near_turn(h)
        coupling_own(2 * h)
        coupling_own(2 * h + 1)

    for copy in coup_copies:
        copy.wait()

    @pl.loop(0, GROUPS // 4)
    def _(h):
        near_turn(GROUPS // 4 + h)
        coupling_halo(0, h)
        coupling_halo(1, h)

    near_sums(GROUPS, inner0, cross0)

    dead = LD + 2 * REACH
    for ref in (c_all, v_all):
        ref[dead] = jnp.zeros(ref.shape[1:], BF16)
    first_half = lower_lanes((FEAT, 128))

    def listed(m):
        u = jnp.transpose(up_pair[m].astype(F32)).astype(BF16)
        tiles, sources = [], []
        for s in range(2):
            leaf = 2 * m + s
            vs, cs = [], []
            for t in range(4):
                picked = []
                for slot in (2 * t, 2 * t + 1):
                    j = coupling_list[slot, leaf]
                    near_by = jnp.clip(j - first + REACH, 0, dead - 1)
                    picked.append(jnp.where(j >= 0, near_by, dead))
                vs.append(jnp.where(first_half, v_all[picked[0]], v_all[picked[1]]))
                cs.append(jnp.where(first_half, c_all[picked[0]], c_all[picked[1]]))
            d2 = dot(u[s * K : (s + 1) * K], jnp.concatenate(vs, axis=1))
            tiles.append(from_square(d2).astype(BF16))
            sources.append(jnp.concatenate(cs, axis=1))
        return jnp.concatenate(sources, axis=0), jnp.concatenate(tiles, axis=0)

    def couple_four(b):
        operands = [listed(b * 4 + s) for s in range(4)]
        for s in range(4):
            product = dot_nt(*operands[s])
            lc[b * 4 + s] = jnp.where(lane_half, product[:R], product[R:])

    def climb(got, width, level0, index):
        coefs = got[:, 0:R, :]
        cen, rad = unpacked_shape(got[:, R : R + 8, :])
        level = level0
        while width > 1:
            two = side_by_side(coefs)
            path_pair[level, pl.ds(0, width // 2)] = two
            path_co[level, pl.ds(0, width // 2)] = pair_coords(cen, rad, units)
            coefs = lift(two)
            cen, rad = merge_shapes(cen, rad)
            width //= 2
            level += 1
        return coefs[0], packed_shape(cen[0], rad[0])

    sub_levels, leaf_levels = ns.bit_length() - 1, nl.bit_length() - 1
    for copy in sub_copies:
        copy.wait()
    top_coef, top_shape = climb(got_sub[...], ns, 0, sub_id)
    for b in range(2):
        couple_four(b)
    root_b[0:R, :] = top_coef
    root_b[R : R + 8, :] = top_shape
    leaf_copies = [
        send(root_b, got_leaf.at[leaf_id], leaf_send.at[o], leaf_recv.at[o], device)
        for o, device in enumerate(leaf_devs)
    ]
    got_leaf[leaf_id] = root_b[...]

    beside = 4
    pl.loop(2, LD // 8 - beside)(couple_four)

    for copy in leaf_copies:
        copy.wait()
    climb(got_leaf[...], nl, sub_levels, leaf_id)

    def masked(pair, side):
        chosen = lower_lanes(pair.shape) == (side == 0)
        return jnp.where(chosen, pair, 0.0)

    held = None
    for level in reversed(range(sub_levels + leaf_levels)):
        position = (sub_id if level < sub_levels else leaf_id)
        shift = level if level < sub_levels else level - sub_levels
        node = position // (2**shift)
        pair = node // 2
        mine = couple_pair(path_pair[level, pair], path_co[level, pair])
        if held is not None:
            mine = mine + dot3(held, down_high, down_low)
        held = masked(mine, lax.rem(node, 2))

    def spread(pair_block):
        n = pair_block.shape[0]
        lower = lower_lanes(pair_block.shape)
        both = jnp.stack(
            [jnp.where(lower, pair_block, 0.0), jnp.where(lower, 0.0, pair_block)], axis=1
        )
        return dot3(both.reshape(2 * n * R, 128), down_high, down_low).reshape(2 * n, R, 128)

    n, offset = 1, LD // 2 - 2
    block = sib[pl.ds(offset, 1)] + dot3(held, down_high, down_low)[None]
    while n < LD // 4:
        block = spread(block)
        n *= 2
        offset -= n
        block = block + sib[pl.ds(offset, n)]
    d1[...] = block
    for b in range(LD // 8 - beside, LD // 8):
        couple_four(b)

    def put_out(b):
        lanes = pl.ds(pl.multiple_of(b * 32 * PT, 32 * PT), 32 * PT)
        return pltpu.make_async_copy(out.at[:, lanes], out_hbm.at[:, lanes], out_sem.at[b])

    @pl.loop(0, LD // 32)
    def _(b):
        below = spread(d1[pl.ds(b * 8, 8)])
        for s in range(16):
            m = b * 16 + s
            coef = lc[m] + below[s]
            stacked = jnp.concatenate(
                [jnp.where(lane_half, coef, 0.0), jnp.where(lane_half, 0.0, coef)], axis=0
            ).astype(BF16)
            far = dot(stacked, basis[pl.ds(2 * m, 2)].reshape(2 * K, PT))
            start = pl.multiple_of(m * 256, 256)
            near = oe[:, pl.ds(pl.multiple_of(GW + m * 256, 256), 256)]
            out[:, pl.ds(start, 256)] = near + jnp.concatenate([far[:R], far[R:]], axis=1)
        put_out(b).start()

    for b in range(LD // 32):
        put_out(b).wait()


def per_device(charges, points, basis, transfer, near_list, coupling_list):
    nl, ns = lax.axis_size("leaf"), lax.axis_size("sub")
    levels = (nl * ns).bit_length() - 1
    widest = max(nl, ns) // 2
    vmem = pl.BlockSpec(memory_space=pltpu.VMEM)
    hbm = pl.BlockSpec(memory_space=pl.ANY)
    total = LD + 2 * REACH + 1

    def body(*refs):
        kernel(nl, ns, *refs)

    dma = pltpu.SemaphoreType.DMA
    return pl.pallas_call(
        body,
        out_shape=jax.ShapeDtypeStruct((R, LD * PT), F32),
        in_specs=[hbm, vmem, hbm, vmem, vmem, pl.BlockSpec(memory_space=pltpu.SMEM)],
        out_specs=hbm,
        scratch_shapes=[
            pltpu.VMEM((LD, K, PT), BF16),
            pltpu.VMEM((R, LD * PT), F32),
            pltpu.VMEM((8, EXT), F32),
            pltpu.VMEM((R, EXT), BF16),
            pltpu.VMEM((R, EXT), F32),
            pltpu.VMEM((FEAT, EXT), BF16),
            pltpu.VMEM((FEAT, EXT), BF16),
            pltpu.VMEM((FEAT, EXT), BF16),
            pltpu.VMEM(((GROUPS + 2) * 128, GW), BF16),
            pltpu.VMEM((GW, GW), BF16),
            pltpu.VMEM((GW, GW), BF16),
            pltpu.VMEM((GW, GW), BF16),
            pltpu.VMEM((GW, GW), BF16),
            pltpu.VMEM((3 * GRP, LD + 16, 128), F32),
            pltpu.VMEM((LD, 8, 128), F32),
            pltpu.VMEM((LD, 8, 128), F32),
            pltpu.VMEM((LD, R, 128), F32),
            pltpu.VMEM((LD // 2, 8, 128), F32),
            pltpu.VMEM((LD // 2, R, 128), F32),
            pltpu.VMEM((LD // 2, FEAT, 128), BF16),
            pltpu.VMEM((total, FEAT, 128), BF16),
            pltpu.VMEM((total, R, 128), BF16),
            pltpu.VMEM((LD // 2, R, 128), F32),
            pltpu.VMEM((LD // 2, R, 128), BF16),
            pltpu.VMEM((2, REACH // 2, R, 128), BF16),
            pltpu.VMEM((16, 128), F32),
            pltpu.VMEM((2, 16, 128), F32),
            pltpu.VMEM((R + 8, 128), F32),
            pltpu.VMEM((ns, R + 8, 128), F32),
            pltpu.VMEM((R + 8, 128), F32),
            pltpu.VMEM((nl, R + 8, 128), F32),
            pltpu.VMEM((levels, widest, R, 128), F32),
            pltpu.VMEM((levels, widest, 8, 128), F32),
            pltpu.VMEM((LD // 4, R, 128), F32),
            dma((4,)), dma((4,)), dma((4,)), dma((4,)),
            dma((ns,)), dma((ns,)), dma((nl,)), dma((nl,)), dma((2,)), dma((LD // 32,)),
        ],
        compiler_params=pltpu.CompilerParams(
            collective_id=0, has_side_effects=True, vmem_limit_bytes=56 * 2**20
        ),
        cost_estimate=pl.CostEstimate(
            flops=6 * 10**9, bytes_accessed=7 * 10**6, transcendentals=4 * 10**7
        ),
    )(charges, points, basis, transfer, near_list.T, coupling_list.T)


def solution(mesh):
    in_specs = (
        P(None, ("leaf", "sub")),
        P(None, ("leaf", "sub")),
        P(("leaf", "sub"), None, None),
        P(),
        P(("leaf", "sub"), None),
        P(("leaf", "sub"), None),
    )
    return jax.shard_map(
        per_device,
        mesh=mesh,
        in_specs=in_specs,
        out_specs=P(None, ("leaf", "sub")),
        check_vma=False,
    )
```
